256 devices in a mesh: tm: 4 (over z_lo, core), height: 64 (over z_hi, y, x).
Axes of the slice: x: 4, y: 4, z: 8 (z_hi: 4, z_lo: 2; z = z_hi * 2 + z_lo), core: 2. Of those that a mesh axis runs over, the one named last changes fastest.
Arguments:
- quantized: bfloat16 [8, 128, 128, 128], P('tm', 'height'), may hold values from -127 to 127
- exponents: int32 [4, 8, 128], P(None, 'tm', 'height'), may hold values from -8 to -5
- out_grad: bfloat16 [8, 128, 128, 128], P('tm', 'height'), may hold values from -6 to 6
- kernel_one: bfloat16 [3, 3, 3, 128, 128], replicated, may hold values from -0.109375 to 0.109375
- kernel_two: bfloat16 [3, 3, 3, 128, 128], replicated, may hold values from -0.109375 to 0.109375
Outputs:
- in_grad: bfloat16 [8, 128, 128, 128], P('tm', 'height')
- kernel_one_grad: float32 [3, 3, 3, 128, 128], replicated
- kernel_two_grad: float32 [3, 3, 3, 128, 128], replicated
The draws below stay inside these ranges and needn't reach their ends.
All inputs are finite; a program needn't handle non-finite values.
Results may differ from the reference program's by a relative error of at most 0.0049.
Values may be sent and summed in bfloat16 or wider, within the bound.
No kernel may reach another device: no remote copies, remote signals or barrier semaphores. Data moves between devices by JAX's collectives and lax.ppermute only.
A program may use at most 64 MiB of HBM per device.

```python
import math
import jax
import jax.numpy as jnp
from jax import lax

C = 128
BLOCK = 32
WIDTH = 128
FRAMES = 8
ROWS = 128


def draw_quantized(key, part):
    key = jax.random.fold_in(key, 11)
    shape = (FRAMES, ROWS, WIDTH, C)
    values = jax.random.randint(key, shape, -127, 128, dtype=jnp.int32)
    return values.astype(jnp.float32).astype(jnp.bfloat16)


def plant(values, stream_key, smallest, high):
    dims = values.shape
    spot = [jax.random.randint(jax.random.fold_in(stream_key, axis), (), 0, dims[axis]) for axis in range(len(dims))]
    values = values.at[tuple(spot)].set(smallest)
    longest = dims.index(max(dims))
    spot[longest] = (spot[longest] + 1) % dims[longest]
    return values.at[tuple(spot)].set(high)


def block_levels(own_key, extent, pieces, least, largest):
    def one(position, shards_of):
        steps = jax.random.uniform(jax.random.fold_in(jax.random.fold_in(own_key, 6), position), (shards_of,), jnp.float32, least / len(pieces), largest / len(pieces))
        return jnp.repeat(jnp.exp(steps), extent[position] // shards_of).reshape((-1,) + (1,) * (len(extent) - position - 1))

    loudness = one(*pieces[0])
    for cut in pieces[1:]:
        loudness = loudness * one(*cut)
    return loudness


def bell_draw(rng, shape, deviation, bound, pieces=(), kind=jnp.bfloat16):
    values = deviation * jax.random.normal(rng, shape, jnp.float32)
    if pieces:
        values = values * block_levels(rng, shape, pieces, -0.22, 0.18)
    return jnp.clip(values, -bound, bound).astype(kind)


def setup_inputs(seed: int = 0) -> dict:
    key_of = jax.random.split(jax.random.key(seed), 6)
    return {
        "quantized": draw_quantized(jax.random.fold_in(key_of[5], 71), 0),
        "exponents": plant(jax.random.randint(key_of[1], (C // BLOCK, FRAMES, ROWS), -8, -4), jax.random.fold_in(key_of[1], 1), -8, (-4) - 1).astype(jnp.int32),
        "out_grad": bell_draw(key_of[2], (FRAMES, ROWS, WIDTH, C), 1.0, 6.0, ((0, 4), (1, 64))),
        "kernel_one": bell_draw(key_of[3], (3, 3, 3, C, C), (27 * C) ** -0.5, 0.109375),
        "kernel_two": bell_draw(key_of[4], (3, 3, 3, C, C), (27 * C) ** -0.5, 0.109375),
    }


def convolve(values, kernel):
    result = lax.conv_general_dilated(values[None], kernel, (1, 1, 1), ((2, 0), (1, 1), (1, 1)), dimension_numbers=('NDHWC', 'DHWIO', 'NDHWC'), precision=lax.Precision.HIGHEST)
    return result[0]

def reference(quantized, exponents, out_grad, kernel_one, kernel_two):
    blocks = C // BLOCK
    scale = jnp.exp2(exponents.astype(jnp.float32))
    scale = jnp.transpose(scale, (1, 2, 0))[:, :, None, :, None]
    codes_float = quantized.astype(jnp.float32).reshape(FRAMES, ROWS, WIDTH, blocks, BLOCK)
    inputs = (codes_float * scale).reshape(FRAMES, ROWS, WIDTH, C).astype(jnp.bfloat16)
    inputs_float = inputs.astype(jnp.float32)
    first_float = kernel_one.astype(jnp.float32)
    second_float = kernel_two.astype(jnp.float32)
    pre = convolve(inputs_float, first_float)
    hidden = jax.nn.silu(pre).astype(jnp.bfloat16)
    unused, pull_two = jax.vjp(convolve, hidden.astype(jnp.float32), second_float)
    hid_grad, two_sum = pull_two(out_grad.astype(jnp.float32))
    sigma = jax.nn.sigmoid(pre)
    pre_grad = (hid_grad * sigma * (1.0 + pre * (1.0 - sigma))).astype(jnp.bfloat16)
    unused_one, pull_one = jax.vjp(convolve, inputs_float, first_float)
    in_grad, one_sum = pull_one(pre_grad.astype(jnp.float32))
    factor = 1.0 / math.sqrt(FRAMES * ROWS * WIDTH)
    return (in_grad.astype(jnp.bfloat16), one_sum * factor, two_sum * factor)
```

```python
import math

import jax
import jax.numpy as jnp
from jax import lax
from jax.experimental import pallas as pl
from jax.experimental.pallas import tpu as pltpu
from jax.sharding import PartitionSpec as P

BF = jnp.bfloat16
F32 = jnp.float32
AXES = ("tm", "height")
TM, HEIGHT = 4, 64
COUNT = TM * HEIGHT
C = 128
ROWS = 27 * C
PART = ROWS // 16


def tm_pairs(first):
    pairs = []
    for tm in range(TM):
        for h in range(HEIGHT):
            if first:
                pairs.append((tm * HEIGHT + h, (tm ^ 1) * HEIGHT + h))
            elif tm in (1, 2):
                pairs.append((tm * HEIGHT + h, (3 - tm) * HEIGHT + h))
            else:
                pairs.append((tm * HEIGHT + h, tm * HEIGHT + (h ^ 1)))
    return pairs


def height_pairs(odd):
    pairs = []
    for tm in range(TM):
        for h in range(HEIGHT):
            up = (h % 2 == 1) if odd else (h % 2 == 0)
            other = h + 1 if up else h - 1
            if 0 <= other < HEIGHT:
                pairs.append((tm * HEIGHT + h, tm * HEIGHT + other))
            else:
                pairs.append((tm * HEIGHT + h, (tm ^ 1) * HEIGHT + h))
    return pairs


def flip_pairs(mask):
    return [(d, d ^ mask) for d in range(COUNT)]


SIBLING = flip_pairs(64)
PLANE = [[base + n for n in range(16)] for base in range(0, COUNT, 16)]


def send(value, pairs):
    return lax.ppermute(value, AXES, pairs)


def exchange(value):
    return lax.all_to_all(value, AXES, 0, 0, axis_index_groups=PLANE, tiled=True)


VMEM = pl.BlockSpec(memory_space=pltpu.VMEM)
SMEM = pl.BlockSpec(memory_space=pltpu.SMEM)
ANY = pl.BlockSpec(memory_space=pl.ANY)


def call(kernel, outs, ins, scratch=(), specs=None, out_specs=None, flops=0, moved=1 << 20, limit=8):
    return pl.pallas_call(
        kernel,
        out_shape=[jax.ShapeDtypeStruct(shape, kind) for shape, kind in outs],
        in_specs=specs or [VMEM] * len(ins),
        out_specs=out_specs or [VMEM] * len(outs),
        scratch_shapes=list(scratch),
        compiler_params=pltpu.CompilerParams(vmem_limit_bytes=limit << 20),
        cost_estimate=pl.CostEstimate(flops=flops, bytes_accessed=moved, transcendentals=0),
    )(*ins)


def columns(value):
    wide = value.astype(F32)
    row = lax.broadcasted_iota(jnp.int32, wide.shape, 0)
    before = jnp.where(row == 0, 0.0, pltpu.roll(wide, 1, 0)).astype(BF)
    after = jnp.where(row == 127, 0.0, pltpu.roll(wide, 127, 0)).astype(BF)
    return before, value, after


def dot(a, b):
    return lax.dot_general(a, b, (((1,), (0,)), ((), ())), preferred_element_type=F32)


def dot_nt(a, b):
    return lax.dot_general(a, b, (((1,), (1,)), ((), ())), preferred_element_type=F32)


def turned(kernel_ref, i, j):
    base = (2 - i) * 9 + (2 - j) * 3
    return jnp.concatenate([kernel_ref[base + 2], kernel_ref[base + 1], kernel_ref[base]], axis=1)


def main_kernel(
    place_ref, near_ref, far_ref, own_ref, grad_ref, one_ref, two_ref,
    keep_ref, away_ref, pre_grad_ref,
    slab_i, slab_g, slab_p, input_t, hidden_t,
):
    core = place_ref[0]

    def margin(t, r, later):
        inside = place_ref[1] < TM - 1 if later else place_ref[1] > 0
        value = jnp.where(core == (0 if later else 1), near_ref[t, r], far_ref[t, r])
        return jnp.where(inside, value, 0).astype(BF)

    for t in range(4):
        for r in range(4):
            value = margin(t, r, False) if t < 2 else own_ref[t - 2, r]
            for k, part in enumerate(columns(value)):
                slab_i[t, r, :, k * C : (k + 1) * C] = part
            flipped = value.T
            if r < 3:
                input_t[t, r, :, 0:C] = flipped
            if r > 0:
                input_t[t, r - 1, :, C : 2 * C] = flipped
            value = grad_ref[t, r] if t < 2 else margin(t - 2, r, True)
            for k, part in enumerate(columns(value)):
                slab_g[t, r, :, k * C : (k + 1) * C] = part
    pre = jnp.zeros((512, C), F32)
    hid = jnp.zeros((512, C), F32)
    for i in range(3):
        for j in range(3):
            pre += dot(slab_i[i : i + 2, j : j + 2].reshape(512, 3 * C), one_ref[i * 3 + j])
            hid += dot_nt(slab_g[i : i + 2, j : j + 2].reshape(512, 3 * C), turned(two_ref, i, j))
    gate = 1.0 / (1.0 + jnp.exp(-pre))
    hidden = (pre * gate).astype(BF)
    pre_grad = (hid * gate * (1.0 + pre * (1.0 - gate))).astype(BF)
    for t in range(2):
        for r in range(2):
            n = 2 * t + r
            hidden_t[:, n * C : (n + 1) * C] = hidden[n * C : (n + 1) * C].T
            value = pre_grad[n * C : (n + 1) * C]
            pre_grad_ref[t, r] = value
            for k, part in enumerate(columns(value)):
                slab_p[t, r * C : (r + 1) * C, k * C : (k + 1) * C] = part

    def store(first, base, value):
        for k in range(3):
            rows = pl.ds((base + 2 - k) * C, C)
            part = value[:, k * C : (k + 1) * C]

            @pl.when(core == first)
            def _():
                keep_ref[rows, :] = part

            @pl.when(core != first)
            def _():
                away_ref[rows, :] = part.astype(BF)

    for i in range(3):
        for j in range(3):
            value = dot(input_t[i, j], slab_p[0]) + dot(input_t[i + 1, j], slab_p[1])
            store(0, i * 9 + j * 3, value)
    for i in range(3):
        for j in range(3):
            value = dot(hidden_t[...], slab_g[i : i + 2, j : j + 2].reshape(512, 3 * C))
            store(1, (2 - i) * 9 + (2 - j) * 3, value)


def in_grad_kernel(place_ref, near_ref, far_ref, own_ref, one_ref, out_ref, slab):
    def later(t, r):
        value = jnp.where(place_ref[0] == 0, near_ref[t, r], far_ref[t, r])
        return jnp.where(place_ref[1] < TM - 1, value, 0).astype(BF)

    for t in range(4):
        for r in range(4):
            value = own_ref[t, r] if t < 2 else later(t - 2, r)
            for k, part in enumerate(columns(value)):
                slab[t, r, :, k * C : (k + 1) * C] = part
    total = jnp.zeros((512, C), F32)
    for i in range(3):
        for j in range(3):
            total += dot_nt(slab[i : i + 2, j : j + 2].reshape(512, 3 * C), turned(one_ref, i, j))
    out_ref[...] = total.astype(BF).reshape(2, 2, C, C)


def body(quantized, exponents, out_grad, kernel_one, kernel_two):
    tm = lax.axis_index("tm")
    index = lax.axis_index("height")
    core = tm % 2
    odd = index % 2 == 1
    where = jnp.stack([core, tm]).astype(jnp.int32)
    one = kernel_one.reshape(27, C, C)
    two = kernel_two.reshape(27, C, C)
    block = (2, 2, C, C)
    scale = jnp.exp2(exponents.astype(F32))
    scale = jnp.repeat(jnp.transpose(scale, (1, 2, 0)), C // 4, axis=2)

    def scaled(codes, powers):
        return (codes.astype(F32) * powers[..., None, :]).astype(BF)

    def met(near, far):
        inside = jnp.where(odd, index < HEIGHT - 1, index > 0)
        far = lax.optimization_barrier(jnp.where(inside, far, 0))
        before = jnp.where(odd, near, far)
        after = jnp.where(odd, far, near)
        return before, after

    def band(before, value, after):
        return jnp.concatenate([before[:, None], value, after[:, None]], axis=1)

    codes = jnp.where(odd, quantized[:, 1], quantized[:, 0])
    powers = jnp.where(odd, scale[:, 1], scale[:, 0])
    edge = jnp.where(odd, out_grad[:, 1], out_grad[:, 0])
    leaving = jnp.concatenate([scaled(codes, powers), edge], axis=0)
    leaving, quantized = lax.optimization_barrier((leaving, quantized))
    far = send(leaving, height_pairs(True))
    inputs = scaled(quantized, scale)
    edge = jnp.where(odd, out_grad[:, 0], out_grad[:, 1])
    leaving = jnp.concatenate([jnp.where(odd, inputs[:, 0], inputs[:, 1]), edge], axis=0)
    inputs, leaving = lax.optimization_barrier((inputs, leaving))
    near = send(leaving, height_pairs(False))
    before, after = met(near, far)
    banded = band(before[:2], inputs, after[:2])
    grad_banded = band(before[2:], out_grad, after[2:])
    near = send(jnp.where(core == 0, banded, grad_banded), tm_pairs(True))
    far = send(jnp.where(core == 0, grad_banded, banded), tm_pairs(False))
    keep, away, pre_grad = call(
        main_kernel,
        [((ROWS, C), F32), ((ROWS, C), BF), (block, BF)],
        [where, near, far, banded, grad_banded, one.reshape(9, 3 * C, C), two],
        specs=[SMEM] + [VMEM] * 6,
        scratch=[
            pltpu.VMEM((4, 4, C, 3 * C), BF),
            pltpu.VMEM((4, 4, C, 3 * C), BF),
            pltpu.VMEM((2, 2 * C, 3 * C), BF),
            pltpu.VMEM((4, 3, C, 2 * C), BF),
            pltpu.VMEM((C, 4 * C), BF),
        ],
        flops=4 * 2 * 27 * C * C * 512,
        limit=32,
    )
    near = send(jnp.where(odd, pre_grad[:, 0], pre_grad[:, 1]), height_pairs(False))
    far = send(jnp.where(odd, pre_grad[:, 1], pre_grad[:, 0]), height_pairs(True))
    before, after = met(near, far)
    total = (keep + send(away, SIBLING).astype(F32)).astype(BF).reshape(16, PART, C)
    total = jnp.sum(exchange(total).astype(F32), axis=0).astype(BF)
    total, before, after = lax.optimization_barrier((total, before, after))
    pre_banded = band(before, pre_grad, after)
    pre_near = send(pre_banded, tm_pairs(True))
    pre_far = send(pre_banded, tm_pairs(False))
    total = total.astype(F32) + send(total, flip_pairs(128)).astype(F32)
    total = total.astype(BF)
    others = [send(total, flip_pairs(16 * n)).astype(F32) for n in (1, 3, 2)]
    factor = 1.0 / math.sqrt(8 * 128 * 128)
    total = (((total.astype(F32) + others[0]) + (others[1] + others[2])) * factor).astype(BF)
    total, pre_near, pre_far = lax.optimization_barrier((total, pre_near, pre_far))
    mine = exchange(jnp.broadcast_to(total[None], (16, PART, C))).reshape(ROWS, C)
    theirs = send(mine, SIBLING)
    one_total = jnp.where(core == 0, mine, theirs).astype(F32)
    two_total = jnp.where(core == 0, theirs, mine).astype(F32)
    (in_grad,) = call(
        in_grad_kernel,
        [(block, BF)],
        [where, pre_near, pre_far, pre_banded, one],
        specs=[SMEM] + [VMEM] * 4,
        scratch=[pltpu.VMEM((4, 4, C, 3 * C), BF)],
        flops=2 * 27 * C * C * 512,
    )
    shape = (3, 3, 3, C, C)
    return (in_grad, one_total.reshape(shape), two_total.reshape(shape))


def solution(mesh):
    placed = (
        P("tm", "height", None, None),
        P(None, "tm", "height"),
        P("tm", "height", None, None),
        P(),
        P(),
    )
    return jax.shard_map(
        body,
        mesh=mesh,
        in_specs=placed,
        out_specs=(P("tm", "height", None, None), P(), P()),
        check_vma=False,
    )
```

```python
import math

import jax
import jax.numpy as jnp
from jax import lax
from jax.experimental import pallas as pl
from jax.experimental.pallas import tpu as pltpu
from jax.sharding import PartitionSpec as P

BF = jnp.bfloat16
F32 = jnp.float32
AXES = ("tm", "height")
TM, HEIGHT = 4, 64
COUNT = TM * HEIGHT
C = 128
ROWS = 27 * C
PART = ROWS // 16


def tm_pairs(first):
    pairs = []
    for tm in range(TM):
        for h in range(HEIGHT):
            if first:
                pairs.append((tm * HEIGHT + h, (tm ^ 1) * HEIGHT + h))
            elif tm in (1, 2):
                pairs.append((tm * HEIGHT + h, (3 - tm) * HEIGHT + h))
            else:
                pairs.append((tm * HEIGHT + h, tm * HEIGHT + (h ^ 1)))
    return pairs


def height_pairs(odd):
    pairs = []
    for tm in range(TM):
        for h in range(HEIGHT):
            up = (h % 2 == 1) if odd else (h % 2 == 0)
            other = h + 1 if up else h - 1
            if 0 <= other < HEIGHT:
                pairs.append((tm * HEIGHT + h, tm * HEIGHT + other))
            else:
                pairs.append((tm * HEIGHT + h, (tm ^ 1) * HEIGHT + h))
    return pairs


def flip_pairs(mask):
    return [(d, d ^ mask) for d in range(COUNT)]


SIBLING = flip_pairs(64)
PLANE = [[base + n for n in range(16)] for base in range(0, COUNT, 16)]


def send(value, pairs):
    return lax.ppermute(value, AXES, pairs)


def exchange(value):
    return lax.all_to_all(value, AXES, 0, 0, axis_index_groups=PLANE, tiled=True)


VMEM = pl.BlockSpec(memory_space=pltpu.VMEM)
SMEM = pl.BlockSpec(memory_space=pltpu.SMEM)
ANY = pl.BlockSpec(memory_space=pl.ANY)


def call(kernel, outs, ins, scratch=(), specs=None, out_specs=None, flops=0, moved=1 << 20, limit=8):
    return pl.pallas_call(
        kernel,
        out_shape=[jax.ShapeDtypeStruct(shape, kind) for shape, kind in outs],
        in_specs=specs or [VMEM] * len(ins),
        out_specs=out_specs or [VMEM] * len(outs),
        scratch_shapes=list(scratch),
        compiler_params=pltpu.CompilerParams(vmem_limit_bytes=limit << 20),
        cost_estimate=pl.CostEstimate(flops=flops, bytes_accessed=moved, transcendentals=0),
    )(*ins)


def columns(value):
    wide = value.astype(F32)
    row = lax.broadcasted_iota(jnp.int32, wide.shape, 0)
    before = jnp.where(row == 0, 0.0, pltpu.roll(wide, 1, 0)).astype(BF)
    after = jnp.where(row == 127, 0.0, pltpu.roll(wide, 127, 0)).astype(BF)
    return before, value, after


def dot(a, b):
    return lax.dot_general(a, b, (((1,), (0,)), ((), ())), preferred_element_type=F32)


def dot_nt(a, b):
    return lax.dot_general(a, b, (((1,), (1,)), ((), ())), preferred_element_type=F32)


def turned(kernel_ref, i, j):
    base = (2 - i) * 9 + (2 - j) * 3
    return jnp.concatenate([kernel_ref[base + 2], kernel_ref[base + 1], kernel_ref[base]], axis=1)


def fill(slab, t, r, value):
    for k, part in enumerate(columns(value)):
        slab[t, r, :, k * C : (k + 1) * C] = part


def fill_turned(turned_ref, t, r, value):
    flipped = value.T
    if r < 3:
        turned_ref[t, r, :, 0:C] = flipped
    if r > 0:
        turned_ref[t, r - 1, :, C : 2 * C] = flipped


def rows_of(slab, frames, j):
    return slab[frames, j : j + 2].reshape(-1, slab.shape[3])


BOTH, FIRST, SECOND = slice(0, 2), slice(0, 1), slice(1, 2)


def own_kernel(
    place_ref, value_ref, margin_ref, one_ref, two_ref,
    turned_ref, pre_ref, hid_ref, slab_i, slab_g,
):
    core = place_ref[0]
    for t in range(2):
        for r in range(4):
            first, second = (
                value_ref[n, t, r - 1] if 0 < r < 3 else margin_ref[n, t, r // 3] for n in range(2)
            )
            fill(slab_i, t, r, first)
            fill(slab_g, t, r, second)
            fill_turned(turned_ref, t, r, jnp.where(core == 0, first, second).astype(BF))
    pre = jnp.zeros((512, C), F32)
    hid = jnp.zeros((512, C), F32)
    pre_1 = jnp.zeros((256, C), F32)
    hid_0 = jnp.zeros((256, C), F32)
    for j in range(3):
        pre += dot(rows_of(slab_i, BOTH, j), one_ref[6 + j])
        pre_1 += dot(rows_of(slab_i, FIRST, j), one_ref[3 + j])
        hid += dot_nt(rows_of(slab_g, BOTH, j), turned(two_ref, 0, j))
        hid_0 += dot_nt(rows_of(slab_g, SECOND, j), turned(two_ref, 1, j))
    pre_ref[0:256] = pre[0:256]
    pre_ref[256:512] = pre[256:512] + pre_1
    hid_ref[0:256] = hid[0:256] + hid_0
    hid_ref[256:512] = hid[256:512]


def pick(own_ref, margin_ref, t, r, *n):
    return own_ref[(*n, t, r - 1)] if 0 < r < 3 else margin_ref[(*n, t, r // 3)]


def rest_kernel(
    place_ref, near_own, near_margin, far_own, far_margin, pre_ref, hid_ref, one_ref, two_ref,
    stay_ref, leave_ref, pre_grad_ref, past_i, later_g,
):
    core = place_ref[0]
    for t in range(2):
        for r in range(4):
            far = pick(far_own, far_margin, t, r)
            value = jnp.where(core == 1, pick(near_own, near_margin, t, r, 0), far)
            fill(past_i, t, r, jnp.where(place_ref[1] > 0, value, 0).astype(BF))
            value = jnp.where(core == 0, pick(near_own, near_margin, t, r, 1), far)
            fill(later_g, t, r, jnp.where(place_ref[1] < TM - 1, value, 0).astype(BF))
    pre = pre_ref[...]
    hid = hid_ref[...]
    pre_0 = jnp.zeros((256, C), F32)
    hid_1 = jnp.zeros((256, C), F32)
    for j in range(3):
        pre += dot(rows_of(past_i, BOTH, j), one_ref[j])
        pre_0 += dot(rows_of(past_i, SECOND, j), one_ref[3 + j])
        hid += dot_nt(rows_of(later_g, BOTH, j), turned(two_ref, 2, j))
        hid_1 += dot_nt(rows_of(later_g, FIRST, j), turned(two_ref, 1, j))
    pre = jnp.concatenate([pre[0:256] + pre_0, pre[256:512]], axis=0)
    hid = jnp.concatenate([hid[0:256], hid[256:512] + hid_1], axis=0)
    gate = 1.0 / (1.0 + jnp.exp(-pre))
    hidden = (pre * gate).astype(BF).reshape(2, 2, C, C)
    pre_grad = (hid * gate * (1.0 + pre * (1.0 - gate))).astype(BF).reshape(2, 2, C, C)
    pre_grad_ref[...] = pre_grad
    stay_ref[...] = jnp.where(core == 0, pre_grad, hidden).astype(BF)
    leave_ref[...] = jnp.where(core == 0, hidden, pre_grad).astype(BF)


def turn_kernel(place_ref, near_own, near_margin, far_own, far_margin, low_ref, high_ref):
    core = place_ref[0]
    inner = (place_ref[1] == 1) | (place_ref[1] == 2)
    for t in range(2):
        for r in range(4):
            far = jnp.where(inner, pick(far_own, far_margin, t, r), 0).astype(BF)
            first = pick(near_own, near_margin, t, r, 0)
            second = pick(near_own, near_margin, t, r, 1)
            fill_turned(low_ref, t, r, jnp.where(core == 0, far, second).astype(BF))
            fill_turned(high_ref, t, r, jnp.where(core == 0, first, far).astype(BF))


def sums_kernel(place_ref, stay_ref, got_ref, low_ref, own_ref, high_ref, out_ref, slab):
    core = place_ref[0]
    for t in range(4):
        for r in range(2):
            early, late = (stay_ref, got_ref) if t < 2 else (got_ref, stay_ref)
            value = jnp.where(core == 0, early[t % 2, r], late[t % 2, r]).astype(BF)
            for k, part in enumerate(columns(value)):
                slab[t, r * C : (r + 1) * C, k * C : (k + 1) * C] = part
    frames = [ref.at[t] for ref in (low_ref, own_ref, high_ref) for t in range(2)]
    for i in range(3):
        total = jnp.zeros((3 * C, 3 * C), F32)
        for t in range(4):
            total += dot(frames[i + t][...].reshape(3 * C, 2 * C), slab[t])
        total = total.astype(BF)
        for j in range(3):
            for k in range(3):
                n = i * 9 + j * 3 + k
                out_ref[n * C : (n + 1) * C, :] = total[j * C : (j + 1) * C, k * C : (k + 1) * C]


def in_grad_kernel(place_ref, near_ref, far_ref, own_ref, one_ref, out_ref, slab):
    def later(t, r):
        value = jnp.where(place_ref[0] == 0, near_ref[t, r], far_ref[t, r])
        return jnp.where(place_ref[1] < TM - 1, value, 0).astype(BF)

    for t in range(4):
        for r in range(4):
            value = own_ref[t, r] if t < 2 else later(t - 2, r)
            for k, part in enumerate(columns(value)):
                slab[t, r, :, k * C : (k + 1) * C] = part
    total = jnp.zeros((512, C), F32)
    for i in range(3):
        for j in range(3):
            total += dot_nt(slab[i : i + 2, j : j + 2].reshape(512, 3 * C), turned(one_ref, i, j))
    out_ref[...] = total.astype(BF).reshape(2, 2, C, C)


def write_kernel(half, place_ref, part_ref, *refs):
    targets, whole, sems = refs[-4:-2], refs[-2], refs[-1]
    third = ROWS // 3

    def copy(kind, i):
        rows = pl.ds(i * third, third)
        return pltpu.make_async_copy(whole.at[rows, :], targets[kind].at[rows, :], sems.at[i])

    for kind in range(2):

        @pl.when(place_ref[0] == (kind + half) % 2)
        def _():
            for i in range(3):
                for j in range(3):
                    for k in range(3):
                        n = (i * 9 + j * 3 + k) * C
                        value = part_ref[n : n + C, :]
                        if kind:
                            m = ((2 - i) * 9 + (2 - j) * 3 + k) * C
                            value = value.T
                        else:
                            m = (i * 9 + j * 3 + 2 - k) * C
                        whole[m : m + C, :] = value.astype(F32)
                copy(kind, 2 - i if kind else i).start()
            for i in range(3):
                copy(kind, i).wait()


def write(half, where, part, targets=()):
    return pl.pallas_call(
        lambda *refs: write_kernel(half, *refs),
        out_shape=[jax.ShapeDtypeStruct((ROWS, C), F32)] * 2,
        in_specs=[SMEM, VMEM] + [ANY] * len(targets),
        out_specs=[ANY, ANY],
        input_output_aliases={2 + n: n for n in range(len(targets))},
        scratch_shapes=[pltpu.VMEM((ROWS, C), F32), pltpu.SemaphoreType.DMA((3,))],
        compiler_params=pltpu.CompilerParams(vmem_limit_bytes=8 << 20),
        cost_estimate=pl.CostEstimate(flops=0, bytes_accessed=3 << 20, transcendentals=0),
    )(where, part, *targets)


def body(quantized, exponents, out_grad, kernel_one, kernel_two):
    tm = lax.axis_index("tm")
    index = lax.axis_index("height")
    core = tm % 2
    odd = index % 2 == 1
    where = jnp.stack([core, tm, index % 2]).astype(jnp.int32)
    one = kernel_one.reshape(27, C, C)
    two = kernel_two.reshape(27, C, C)
    nine = one.reshape(9, 3 * C, C)
    block = (2, 2, C, C)

    def met(near, far):
        inside = jnp.where(odd, index < HEIGHT - 1, index > 0)
        far = lax.optimization_barrier(jnp.where(inside, far, 0))
        before = jnp.where(odd, near, far)
        after = jnp.where(odd, far, near)
        return before, after

    def band(before, value, after):
        return jnp.concatenate([before[:, None], value, after[:, None]], axis=1)

    scale = jnp.exp2(exponents.astype(F32))
    scale = jnp.repeat(jnp.transpose(scale, (1, 2, 0)), C // 4, axis=2)
    scale = jnp.stack([scale, jnp.ones_like(scale)])[:, :, :, None, :]
    both = lax.optimization_barrier(jnp.stack([quantized, out_grad]))
    both = (both.astype(F32) * scale).astype(BF)
    pair = (4, C, C)
    near = send(jnp.where(odd, both[:, :, 0], both[:, :, 1]).reshape(pair), height_pairs(False))
    far = send(jnp.where(odd, both[:, :, 1], both[:, :, 0]).reshape(pair), height_pairs(True))
    near_own = send(both, tm_pairs(True))
    far_own = send(jnp.where(core == 0, both[1], both[0]), tm_pairs(False))
    before, after = met(near, far)
    margin = jnp.stack([before.reshape(2, 2, C, C), after.reshape(2, 2, C, C)], axis=2)
    near_margin = send(margin, tm_pairs(True))
    far_margin = send(jnp.where(core == 0, margin[1], margin[0]), tm_pairs(False))
    slab = (2, 4, C, 3 * C)
    flipped = (2, 3, C, 2 * C)
    half = 2 * 27 * C * C * 512
    middle, pre, hid = call(
        own_kernel,
        [(flipped, BF), ((512, C), F32), ((512, C), F32)],
        [where, both, margin, nine, two],
        specs=[SMEM] + [VMEM] * 4,
        scratch=[pltpu.VMEM(slab, BF), pltpu.VMEM(slab, BF)],
        flops=half,
        limit=16,
    )
    beside = [near_own, near_margin, far_own, far_margin]
    stay, leave, pre_grad = call(
        rest_kernel,
        [(block, BF)] * 3,
        [where, *beside, pre, hid, nine, two],
        specs=[SMEM] + [VMEM] * 8,
        scratch=[pltpu.VMEM(slab, BF), pltpu.VMEM(slab, BF)],
        flops=half,
        limit=16,
    )
    low, high = call(
        turn_kernel,
        [(flipped, BF)] * 2,
        [where, *beside],
        specs=[SMEM] + [VMEM] * 4,
        limit=16,
    )
    got = send(leave, SIBLING)
    (total,) = call(
        sums_kernel,
        [((ROWS, C), BF)],
        [where, stay, got, low, middle, high],
        specs=[SMEM] + [VMEM] * 5,
        scratch=[pltpu.VMEM((4, 2 * C, 3 * C), BF)],
        flops=2 * half,
        limit=16,
    )
    near = send(jnp.where(odd, pre_grad[:, 0], pre_grad[:, 1]), height_pairs(False))
    far = send(jnp.where(odd, pre_grad[:, 1], pre_grad[:, 0]), height_pairs(True))
    before, after = met(near, far)
    total = jnp.sum(exchange(total.reshape(16, PART, C)).astype(F32), axis=0).astype(BF)
    total, before, after = lax.optimization_barrier((total, before, after))
    pre_banded = band(before, pre_grad, after)
    pre_near = send(pre_banded, tm_pairs(True))
    pre_far = send(pre_banded, tm_pairs(False))
    total = total.astype(F32) + send(total, flip_pairs(128)).astype(F32)
    total = total.astype(BF)
    others = [send(total, flip_pairs(16 * n)).astype(F32) for n in (1, 3, 2)]
    factor = 1.0 / math.sqrt(8 * 128 * 128)
    total = (((total.astype(F32) + others[0]) + (others[1] + others[2])) * factor).astype(BF)
    total, pre_near, pre_far = lax.optimization_barrier((total, pre_near, pre_far))
    mine = exchange(jnp.broadcast_to(total[None], (16, PART, C))).reshape(ROWS, C)
    (in_grad,) = call(
        in_grad_kernel,
        [(block, BF)],
        [where, pre_near, pre_far, pre_banded, one],
        specs=[SMEM] + [VMEM] * 4,
        scratch=[pltpu.VMEM((4, 4, C, 3 * C), BF)],
        flops=2 * 27 * C * C * 512,
    )
    mine, in_grad = lax.optimization_barrier((mine, in_grad))
    theirs = send(mine, SIBLING)
    totals = write(0, where, mine)
    one_total, two_total = write(1, where, theirs, totals)
    shape = (3, 3, 3, C, C)
    return (in_grad, one_total.reshape(shape), two_total.reshape(shape))


def solution(mesh):
    placed = (
        P("tm", "height", None, None),
        P(None, "tm", "height"),
        P("tm", "height", None, None),
        P(),
        P(),
    )
    return jax.shard_map(
        body,
        mesh=mesh,
        in_specs=placed,
        out_specs=(P("tm", "height", None, None), P(), P()),
        check_vma=False,
    )
```

```python
import math

import jax
import jax.numpy as jnp
from jax import lax
from jax.experimental import pallas as pl
from jax.experimental.pallas import tpu as pltpu
from jax.sharding import PartitionSpec as P

BF = jnp.bfloat16
F32 = jnp.float32
AXES = ("tm", "height")
TM, HEIGHT = 4, 64
COUNT = TM * HEIGHT
C = 128
ROWS = 27 * C
PART = ROWS // 16


def tm_pairs(first):
    pairs = []
    for tm in range(TM):
        for h in range(HEIGHT):
            if first:
                pairs.append((tm * HEIGHT + h, (tm ^ 1) * HEIGHT + h))
            elif tm in (1, 2):
                pairs.append((tm * HEIGHT + h, (3 - tm) * HEIGHT + h))
            else:
                pairs.append((tm * HEIGHT + h, tm * HEIGHT + (h ^ 1)))
    return pairs


def height_pairs(odd):
    pairs = []
    for tm in range(TM):
        for h in range(HEIGHT):
            up = (h % 2 == 1) if odd else (h % 2 == 0)
            other = h + 1 if up else h - 1
            if 0 <= other < HEIGHT:
                pairs.append((tm * HEIGHT + h, tm * HEIGHT + other))
            else:
                pairs.append((tm * HEIGHT + h, (tm ^ 1) * HEIGHT + h))
    return pairs


def flip_pairs(mask):
    return [(d, d ^ mask) for d in range(COUNT)]


SIBLING = flip_pairs(64)
PLANE = [[base + (n + 10) % 16 for n in range(16)] for base in range(0, COUNT, 16)]


def send(value, pairs):
    return lax.ppermute(value, AXES, pairs)


def exchange(value):
    return lax.all_to_all(value, AXES, 0, 0, axis_index_groups=PLANE, tiled=True)


VMEM = pl.BlockSpec(memory_space=pltpu.VMEM)
SMEM = pl.BlockSpec(memory_space=pltpu.SMEM)
ANY = pl.BlockSpec(memory_space=pl.ANY)


def call(kernel, outs, ins, scratch=(), specs=None, out_specs=None, flops=0, moved=1 << 20, limit=8):
    return pl.pallas_call(
        kernel,
        out_shape=[jax.ShapeDtypeStruct(shape, kind) for shape, kind in outs],
        in_specs=specs or [VMEM] * len(ins),
        out_specs=out_specs or [VMEM] * len(outs),
        scratch_shapes=list(scratch),
        compiler_params=pltpu.CompilerParams(vmem_limit_bytes=limit << 20),
        cost_estimate=pl.CostEstimate(flops=flops, bytes_accessed=moved, transcendentals=0),
    )(*ins)


def columns(value):
    wide = value.astype(F32)
    row = lax.broadcasted_iota(jnp.int32, wide.shape, 0)
    before = jnp.where(row == 0, 0.0, pltpu.roll(wide, 1, 0)).astype(BF)
    after = jnp.where(row == 127, 0.0, pltpu.roll(wide, 127, 0)).astype(BF)
    return before, value, after


def dot(a, b):
    return lax.dot_general(a, b, (((1,), (0,)), ((), ())), preferred_element_type=F32)


def dot_nt(a, b):
    return lax.dot_general(a, b, (((1,), (1,)), ((), ())), preferred_element_type=F32)


def turned(kernel_ref, i, j):
    base = (2 - i) * 9 + (2 - j) * 3
    return jnp.concatenate([kernel_ref[base + 2], kernel_ref[base + 1], kernel_ref[base]], axis=1)


def fill(slab, t, r, value):
    for k, part in enumerate(columns(value)):
        slab[t, r, :, k * C : (k + 1) * C] = part


def fill_turned(turned_ref, t, r, value):
    flipped = value.T
    if r < 3:
        turned_ref[t, r, :, 0:C] = flipped
    if r > 0:
        turned_ref[t, r - 1, :, C : 2 * C] = flipped


def rows_of(slab, frames, j):
    return slab[frames, j : j + 2].reshape(-1, slab.shape[3])


BOTH, FIRST, SECOND = slice(0, 2), slice(0, 1), slice(1, 2)


def own_kernel(
    place_ref, value_ref, margin_ref, one_ref, two_ref,
    turned_ref, pre_ref, hid_ref, slab_i, slab_g,
):
    core = place_ref[0]
    for t in range(2):
        for r in range(4):
            first, second = (
                value_ref[n, t, r - 1] if 0 < r < 3 else margin_ref[n, t, r // 3] for n in range(2)
            )
            fill(slab_i, t, r, first)
            fill(slab_g, t, r, second)
            fill_turned(turned_ref, t, r, jnp.where(core == 0, first, second).astype(BF))
    pre = jnp.zeros((512, C), F32)
    hid = jnp.zeros((512, C), F32)
    pre_1 = jnp.zeros((256, C), F32)
    hid_0 = jnp.zeros((256, C), F32)
    for j in range(3):
        pre += dot(rows_of(slab_i, BOTH, j), one_ref[6 + j])
        pre_1 += dot(rows_of(slab_i, FIRST, j), one_ref[3 + j])
        hid += dot_nt(rows_of(slab_g, BOTH, j), turned(two_ref, 0, j))
        hid_0 += dot_nt(rows_of(slab_g, SECOND, j), turned(two_ref, 1, j))
    pre_ref[0:256] = pre[0:256]
    pre_ref[256:512] = pre[256:512] + pre_1
    hid_ref[0:256] = hid[0:256] + hid_0
    hid_ref[256:512] = hid[256:512]


def pick(own_ref, margin_ref, t, r, *n):
    return own_ref[(*n, t, r - 1)] if 0 < r < 3 else margin_ref[(*n, t, r // 3)]


def rest_kernel(
    place_ref, near_own, near_margin, far_own, far_margin, pre_ref, hid_ref, one_ref, two_ref,
    stay_ref, leave_ref, pre_grad_ref, past_i, later_g,
):
    core = place_ref[0]
    for t in range(2):
        for r in range(4):
            far = pick(far_own, far_margin, t, r)
            value = jnp.where(core == 1, pick(near_own, near_margin, t, r, 0), far)
            fill(past_i, t, r, jnp.where(place_ref[1] > 0, value, 0).astype(BF))
            value = jnp.where(core == 0, pick(near_own, near_margin, t, r, 1), far)
            fill(later_g, t, r, jnp.where(place_ref[1] < TM - 1, value, 0).astype(BF))
    pre = pre_ref[...]
    hid = hid_ref[...]
    pre_0 = jnp.zeros((256, C), F32)
    hid_1 = jnp.zeros((256, C), F32)
    for j in range(3):
        pre += dot(rows_of(past_i, BOTH, j), one_ref[j])
        pre_0 += dot(rows_of(past_i, SECOND, j), one_ref[3 + j])
        hid += dot_nt(rows_of(later_g, BOTH, j), turned(two_ref, 2, j))
        hid_1 += dot_nt(rows_of(later_g, FIRST, j), turned(two_ref, 1, j))
    pre = jnp.concatenate([pre[0:256] + pre_0, pre[256:512]], axis=0)
    hid = jnp.concatenate([hid[0:256], hid[256:512] + hid_1], axis=0)
    gate = 1.0 / (1.0 + jnp.exp(-pre))
    hidden = (pre * gate).astype(BF).reshape(2, 2, C, C)
    pre_grad = (hid * gate * (1.0 + pre * (1.0 - gate))).astype(BF).reshape(2, 2, C, C)
    pre_grad_ref[...] = pre_grad
    stay_ref[...] = jnp.where(core == 0, pre_grad, hidden).astype(BF)
    leave_ref[...] = jnp.where(core == 0, hidden, pre_grad).astype(BF)


def turn_kernel(place_ref, near_own, near_margin, far_own, far_margin, low_ref, high_ref):
    core = place_ref[0]
    inner = (place_ref[1] == 1) | (place_ref[1] == 2)
    for t in range(2):
        for r in range(4):
            far = jnp.where(inner, pick(far_own, far_margin, t, r), 0).astype(BF)
            first = pick(near_own, near_margin, t, r, 0)
            second = pick(near_own, near_margin, t, r, 1)
            fill_turned(low_ref, t, r, jnp.where(core == 0, far, second).astype(BF))
            fill_turned(high_ref, t, r, jnp.where(core == 0, first, far).astype(BF))


def sums_kernel(place_ref, stay_ref, got_ref, low_ref, own_ref, high_ref, out_ref, slab):
    core = place_ref[0]
    for t in range(4):
        for r in range(2):
            early, late = (stay_ref, got_ref) if t < 2 else (got_ref, stay_ref)
            value = jnp.where(core == 0, early[t % 2, r], late[t % 2, r]).astype(BF)
            for k, part in enumerate(columns(value)):
                slab[t, r * C : (r + 1) * C, k * C : (k + 1) * C] = part
    frames = [ref.at[t] for ref in (low_ref, own_ref, high_ref) for t in range(2)]
    for i in range(3):
        total = jnp.zeros((3 * C, 3 * C), F32)
        for t in range(4):
            total += dot(frames[i + t][...].reshape(3 * C, 2 * C), slab[t])
        total = total.astype(BF)
        for j in range(3):
            for k in range(3):
                n = i * 9 + j * 3 + k
                out_ref[n * C : (n + 1) * C, :] = total[j * C : (j + 1) * C, k * C : (k + 1) * C]


def in_grad_kernel(place_ref, near_ref, far_ref, own_ref, one_ref, out_ref, slab):
    def later(t, r):
        value = jnp.where(place_ref[0] == 0, near_ref[t, r], far_ref[t, r])
        return jnp.where(place_ref[1] < TM - 1, value, 0).astype(BF)

    for t in range(4):
        for r in range(4):
            value = own_ref[t, r] if t < 2 else later(t - 2, r)
            for k, part in enumerate(columns(value)):
                slab[t, r, :, k * C : (k + 1) * C] = part
    total = jnp.zeros((512, C), F32)
    for i in range(3):
        for j in range(3):
            total += dot_nt(slab[i : i + 2, j : j + 2].reshape(512, 3 * C), turned(one_ref, i, j))
    out_ref[...] = total.astype(BF).reshape(2, 2, C, C)


def write_kernel(half, place_ref, part_ref, *refs):
    targets, whole, sems = refs[-4:-2], refs[-2], refs[-1]
    third = ROWS // 3

    def copy(kind, i):
        rows = pl.ds(i * third, third)
        return pltpu.make_async_copy(whole.at[rows, :], targets[kind].at[rows, :], sems.at[i])

    for kind in range(2):

        @pl.when(place_ref[0] == (kind + half) % 2)
        def _():
            for i in range(3):
                for j in range(3):
                    for k in range(3):
                        n = (i * 9 + j * 3 + k) * C
                        value = part_ref[n : n + C, :]
                        if kind:
                            m = ((2 - i) * 9 + (2 - j) * 3 + k) * C
                            value = value.T
                        else:
                            m = (i * 9 + j * 3 + 2 - k) * C
                        whole[m : m + C, :] = value.astype(F32)
                copy(kind, 2 - i if kind else i).start()
            for i in range(3):
                copy(kind, i).wait()


def write(half, where, part, targets=()):
    return pl.pallas_call(
        lambda *refs: write_kernel(half, *refs),
        out_shape=[jax.ShapeDtypeStruct((ROWS, C), F32)] * 2,
        in_specs=[SMEM, VMEM] + [ANY] * len(targets),
        out_specs=[ANY, ANY],
        input_output_aliases={2 + n: n for n in range(len(targets))},
        scratch_shapes=[pltpu.VMEM((ROWS, C), F32), pltpu.SemaphoreType.DMA((3,))],
        compiler_params=pltpu.CompilerParams(vmem_limit_bytes=8 << 20),
        cost_estimate=pl.CostEstimate(flops=0, bytes_accessed=3 << 20, transcendentals=0),
    )(where, part, *targets)


def body(quantized, exponents, out_grad, kernel_one, kernel_two):
    tm = lax.axis_index("tm")
    index = lax.axis_index("height")
    core = tm % 2
    odd = index % 2 == 1
    where = jnp.stack([core, tm, index % 2]).astype(jnp.int32)
    one = kernel_one.reshape(27, C, C)
    two = kernel_two.reshape(27, C, C)
    nine = one.reshape(9, 3 * C, C)
    block = (2, 2, C, C)

    def met(near, far):
        inside = jnp.where(odd, index < HEIGHT - 1, index > 0)
        far = lax.optimization_barrier(jnp.where(inside, far, 0))
        before = jnp.where(odd, near, far)
        after = jnp.where(odd, far, near)
        return before, after

    def band(before, value, after):
        return jnp.concatenate([before[:, None], value, after[:, None]], axis=1)

    scale = jnp.exp2(exponents.astype(F32))
    scale = jnp.repeat(jnp.transpose(scale, (1, 2, 0)), C // 4, axis=2)
    scale = jnp.stack([scale, jnp.ones_like(scale)])[:, :, :, None, :]
    both = lax.optimization_barrier(jnp.stack([quantized, out_grad]))
    both = (both.astype(F32) * scale).astype(BF)
    pair = (4, C, C)
    near = send(jnp.where(odd, both[:, :, 0], both[:, :, 1]).reshape(pair), height_pairs(False))
    far = send(jnp.where(odd, both[:, :, 1], both[:, :, 0]).reshape(pair), height_pairs(True))
    near_own = send(both, tm_pairs(True))
    far_own = send(jnp.where(core == 0, both[1], both[0]), tm_pairs(False))
    before, after = met(near, far)
    margin = jnp.stack([before.reshape(2, 2, C, C), after.reshape(2, 2, C, C)], axis=2)
    near_margin = send(margin, tm_pairs(True))
    far_margin = send(jnp.where(core == 0, margin[1], margin[0]), tm_pairs(False))
    slab = (2, 4, C, 3 * C)
    flipped = (2, 3, C, 2 * C)
    half = 2 * 27 * C * C * 512
    middle, pre, hid = call(
        own_kernel,
        [(flipped, BF), ((512, C), F32), ((512, C), F32)],
        [where, both, margin, nine, two],
        specs=[SMEM] + [VMEM] * 4,
        scratch=[pltpu.VMEM(slab, BF), pltpu.VMEM(slab, BF)],
        flops=half,
        limit=16,
    )
    beside = [near_own, near_margin, far_own, far_margin]
    stay, leave, pre_grad = call(
        rest_kernel,
        [(block, BF)] * 3,
        [where, *beside, pre, hid, nine, two],
        specs=[SMEM] + [VMEM] * 8,
        scratch=[pltpu.VMEM(slab, BF), pltpu.VMEM(slab, BF)],
        flops=half,
        limit=16,
    )
    low, high = call(
        turn_kernel,
        [(flipped, BF)] * 2,
        [where, *beside],
        specs=[SMEM] + [VMEM] * 4,
        limit=16,
    )
    got = send(leave, SIBLING)
    (total,) = call(
        sums_kernel,
        [((ROWS, C), BF)],
        [where, stay, got, low, middle, high],
        specs=[SMEM] + [VMEM] * 5,
        scratch=[pltpu.VMEM((4, 2 * C, 3 * C), BF)],
        flops=2 * half,
        limit=16,
    )
    near = send(jnp.where(odd, pre_grad[:, 0], pre_grad[:, 1]), height_pairs(False))
    far = send(jnp.where(odd, pre_grad[:, 1], pre_grad[:, 0]), height_pairs(True))
    before, after = met(near, far)
    total = jnp.sum(exchange(total.reshape(16, PART, C)).astype(F32), axis=0).astype(BF)
    total, before, after = lax.optimization_barrier((total, before, after))
    pre_banded = band(before, pre_grad, after)
    pre_near = send(pre_banded, tm_pairs(True))
    pre_far = send(pre_banded, tm_pairs(False))
    other = send(total, flip_pairs(128))
    total = total.astype(F32) + other.astype(F32)
    total = total.astype(BF)
    others = [send(total, flip_pairs(16 * n)) for n in (1, 3, 2)]
    (in_grad,) = call(
        in_grad_kernel,
        [(block, BF)],
        [where, pre_near, pre_far, pre_banded, one],
        specs=[SMEM] + [VMEM] * 4,
        scratch=[pltpu.VMEM((4, 4, C, 3 * C), BF)],
        flops=2 * 27 * C * C * 512,
    )
    others, in_grad = lax.optimization_barrier((others, in_grad))
    total, *others = (part.astype(F32) for part in (total, *others))
    factor = 1.0 / math.sqrt(8 * 128 * 128)
    total = (((total + others[0]) + (others[1] + others[2])) * factor).astype(BF)
    mine = exchange(jnp.broadcast_to(total[None], (16, PART, C))).reshape(ROWS, C)
    theirs = send(mine, SIBLING)
    totals = write(0, where, mine)
    one_total, two_total = write(1, where, theirs, totals)
    shape = (3, 3, 3, C, C)
    return (in_grad, one_total.reshape(shape), two_total.reshape(shape))


def solution(mesh):
    placed = (
        P("tm", "height", None, None),
        P(None, "tm", "height"),
        P("tm", "height", None, None),
        P(),
        P(),
    )
    return jax.shard_map(
        body,
        mesh=mesh,
        in_specs=placed,
        out_specs=(P("tm", "height", None, None), P(), P()),
        check_vma=False,
    )
```

```python
import math

import jax
import jax.numpy as jnp
from jax import lax
from jax.experimental import pallas as pl
from jax.experimental.pallas import tpu as pltpu
from jax.sharding import PartitionSpec as P

BF = jnp.bfloat16
F32 = jnp.float32
AXES = ("tm", "height")
TM, HEIGHT = 4, 64
COUNT = TM * HEIGHT
C = 128
ROWS = 27 * C
PART = ROWS // 16


def tm_pairs(first):
    pairs = []
    for tm in range(TM):
        for h in range(HEIGHT):
            if first:
                pairs.append((tm * HEIGHT + h, (tm ^ 1) * HEIGHT + h))
            elif tm in (1, 2):
                pairs.append((tm * HEIGHT + h, (3 - tm) * HEIGHT + h))
            else:
                pairs.append((tm * HEIGHT + h, tm * HEIGHT + (h ^ 1)))
    return pairs


def height_pairs(odd):
    pairs = []
    for tm in range(TM):
        for h in range(HEIGHT):
            up = (h % 2 == 1) if odd else (h % 2 == 0)
            other = h + 1 if up else h - 1
            if 0 <= other < HEIGHT:
                pairs.append((tm * HEIGHT + h, tm * HEIGHT + other))
            else:
                pairs.append((tm * HEIGHT + h, (tm ^ 1) * HEIGHT + h))
    return pairs


def flip_pairs(mask):
    return [(d, d ^ mask) for d in range(COUNT)]


SIBLING = flip_pairs(64)
PLANE = [[base + (n + 10) % 16 for n in range(16)] for base in range(0, COUNT, 16)]


def send(value, pairs):
    return lax.ppermute(value, AXES, pairs)


def exchange(value):
    return lax.all_to_all(value, AXES, 0, 0, axis_index_groups=PLANE, tiled=True)


VMEM = pl.BlockSpec(memory_space=pltpu.VMEM)
SMEM = pl.BlockSpec(memory_space=pltpu.SMEM)
ANY = pl.BlockSpec(memory_space=pl.ANY)


def call(kernel, outs, ins, scratch=(), specs=None, out_specs=None, flops=0, moved=1 << 20, limit=8):
    return pl.pallas_call(
        kernel,
        out_shape=[jax.ShapeDtypeStruct(shape, kind) for shape, kind in outs],
        in_specs=specs or [VMEM] * len(ins),
        out_specs=out_specs or [VMEM] * len(outs),
        scratch_shapes=list(scratch),
        compiler_params=pltpu.CompilerParams(vmem_limit_bytes=limit << 20),
        cost_estimate=pl.CostEstimate(flops=flops, bytes_accessed=moved, transcendentals=0),
    )(*ins)


def columns(value):
    wide = value.astype(F32)
    row = lax.broadcasted_iota(jnp.int32, wide.shape, 0)
    before = jnp.where(row == 0, 0.0, pltpu.roll(wide, 1, 0)).astype(BF)
    after = jnp.where(row == 127, 0.0, pltpu.roll(wide, 127, 0)).astype(BF)
    return before, value, after


def dot(a, b):
    return lax.dot_general(a, b, (((1,), (0,)), ((), ())), preferred_element_type=F32)


def dot_nt(a, b):
    return lax.dot_general(a, b, (((1,), (1,)), ((), ())), preferred_element_type=F32)


def turned(kernel_ref, i, j):
    base = (2 - i) * 9 + (2 - j) * 3
    return jnp.concatenate([kernel_ref[base + 2], kernel_ref[base + 1], kernel_ref[base]], axis=1)


def fill(slab, t, r, value):
    for k, part in enumerate(columns(value)):
        slab[t, r, :, k * C : (k + 1) * C] = part


def fill_turned(turned_ref, t, r, value):
    flipped = value.T
    if r < 3:
        turned_ref[t, r, :, 0:C] = flipped
    if r > 0:
        turned_ref[t, r - 1, :, C : 2 * C] = flipped


def rows_of(slab, frames, j):
    return slab[frames, j : j + 2].reshape(-1, slab.shape[3])


BOTH, FIRST, SECOND = slice(0, 2), slice(0, 1), slice(1, 2)


def own_kernel(
    place_ref, value_ref, margin_ref, one_ref, two_ref,
    turned_ref, pre_ref, hid_ref, slab_i, slab_g,
):
    core = place_ref[0]
    for t in range(2):
        for r in range(4):
            first, second = (
                value_ref[n, t, r - 1] if 0 < r < 3 else margin_ref[n, t, r // 3] for n in range(2)
            )
            fill(slab_i, t, r, first)
            fill(slab_g, t, r, second)
            fill_turned(turned_ref, t, r, jnp.where(core == 0, first, second).astype(BF))
    pre = jnp.zeros((512, C), F32)
    hid = jnp.zeros((512, C), F32)
    pre_1 = jnp.zeros((256, C), F32)
    hid_0 = jnp.zeros((256, C), F32)
    for j in range(3):
        pre += dot(rows_of(slab_i, BOTH, j), one_ref[6 + j])
        pre_1 += dot(rows_of(slab_i, FIRST, j), one_ref[3 + j])
        hid += dot_nt(rows_of(slab_g, BOTH, j), turned(two_ref, 0, j))
        hid_0 += dot_nt(rows_of(slab_g, SECOND, j), turned(two_ref, 1, j))
    pre_ref[0:256] = pre[0:256]
    pre_ref[256:512] = pre[256:512] + pre_1
    hid_ref[0:256] = hid[0:256] + hid_0
    hid_ref[256:512] = hid[256:512]


def pick(own_ref, margin_ref, t, r, *n):
    return own_ref[(*n, t, r - 1)] if 0 < r < 3 else margin_ref[(*n, t, r // 3)]


def rest_kernel(
    place_ref, near_own, near_margin, far_own, far_margin, pre_ref, hid_ref, one_ref, two_ref,
    stay_ref, leave_ref, pre_grad_ref, past_i, later_g,
):
    core = place_ref[0]
    for t in range(2):
        for r in range(4):
            far = pick(far_own, far_margin, t, r)
            value = jnp.where(core == 1, pick(near_own, near_margin, t, r, 0), far)
            fill(past_i, t, r, jnp.where(place_ref[1] > 0, value, 0).astype(BF))
            value = jnp.where(core == 0, pick(near_own, near_margin, t, r, 1), far)
            fill(later_g, t, r, jnp.where(place_ref[1] < TM - 1, value, 0).astype(BF))
    pre = pre_ref[...]
    hid = hid_ref[...]
    pre_0 = jnp.zeros((256, C), F32)
    hid_1 = jnp.zeros((256, C), F32)
    for j in range(3):
        pre += dot(rows_of(past_i, BOTH, j), one_ref[j])
        pre_0 += dot(rows_of(past_i, SECOND, j), one_ref[3 + j])
        hid += dot_nt(rows_of(later_g, BOTH, j), turned(two_ref, 2, j))
        hid_1 += dot_nt(rows_of(later_g, FIRST, j), turned(two_ref, 1, j))
    pre = jnp.concatenate([pre[0:256] + pre_0, pre[256:512]], axis=0)
    hid = jnp.concatenate([hid[0:256], hid[256:512] + hid_1], axis=0)
    gate = 1.0 / (1.0 + jnp.exp(-pre))
    hidden = (pre * gate).astype(BF).reshape(2, 2, C, C)
    pre_grad = (hid * gate * (1.0 + pre * (1.0 - gate))).astype(BF).reshape(2, 2, C, C)
    pre_grad_ref[...] = pre_grad
    stay_ref[...] = jnp.where(core == 0, pre_grad, hidden).astype(BF)
    leave_ref[...] = jnp.where(core == 0, hidden, pre_grad).astype(BF)


def turn_kernel(place_ref, near_own, near_margin, far_own, far_margin, low_ref, high_ref):
    core = place_ref[0]
    inner = (place_ref[1] == 1) | (place_ref[1] == 2)
    for t in range(2):
        for r in range(4):
            far = jnp.where(inner, pick(far_own, far_margin, t, r), 0).astype(BF)
            first = pick(near_own, near_margin, t, r, 0)
            second = pick(near_own, near_margin, t, r, 1)
            fill_turned(low_ref, t, r, jnp.where(core == 0, far, second).astype(BF))
            fill_turned(high_ref, t, r, jnp.where(core == 0, first, far).astype(BF))


def sums_kernel(place_ref, stay_ref, got_ref, low_ref, own_ref, high_ref, out_hbm, slab, out_ref, sems):
    core = place_ref[0]
    for t in range(4):
        for r in range(2):
            early, late = (stay_ref, got_ref) if t < 2 else (got_ref, stay_ref)
            value = jnp.where(core == 0, early[t % 2, r], late[t % 2, r]).astype(BF)
            for k, part in enumerate(columns(value)):
                slab[t, r * C : (r + 1) * C, k * C : (k + 1) * C] = part
    frames = [ref.at[t] for ref in (low_ref, own_ref, high_ref) for t in range(2)]
    copies = []
    for i in range(3):
        total = jnp.zeros((3 * C, 3 * C), F32)
        for t in range(4):
            total += dot(frames[i + t][...].reshape(3 * C, 2 * C), slab[t])
        total = total.astype(BF)
        for j in range(3):
            for k in range(3):
                n = i * 9 + j * 3 + k
                out_ref[n * C : (n + 1) * C, :] = total[j * C : (j + 1) * C, k * C : (k + 1) * C]
        rows = pl.ds(i * (ROWS // 3), ROWS // 3)
        copies.append(pltpu.make_async_copy(out_ref.at[rows, :], out_hbm.at[rows, :], sems.at[i]))
        copies[-1].start()
    for copy in copies:
        copy.wait()


def in_grad_kernel(place_ref, near_ref, far_ref, own_ref, one_ref, out_ref, slab):
    def later(t, r):
        value = jnp.where(place_ref[0] == 0, near_ref[t, r], far_ref[t, r])
        return jnp.where(place_ref[1] < TM - 1, value, 0).astype(BF)

    for t in range(4):
        for r in range(4):
            value = own_ref[t, r] if t < 2 else later(t - 2, r)
            for k, part in enumerate(columns(value)):
                slab[t, r, :, k * C : (k + 1) * C] = part
    total = jnp.zeros((512, C), F32)
    for i in range(3):
        for j in range(3):
            total += dot_nt(slab[i : i + 2, j : j + 2].reshape(512, 3 * C), turned(one_ref, i, j))
    out_ref[...] = total.astype(BF).reshape(2, 2, C, C)


def write_kernel(half, place_ref, part_ref, *refs):
    targets, whole, sems = refs[-4:-2], refs[-2], refs[-1]
    third = ROWS // 3

    def copy(kind, i):
        rows = pl.ds(i * third, third)
        return pltpu.make_async_copy(whole.at[rows, :], targets[kind].at[rows, :], sems.at[i])

    for kind in range(2):

        @pl.when(place_ref[0] == (kind + half) % 2)
        def _():
            for i in range(3):
                for j in range(3):
                    for k in range(3):
                        n = (i * 9 + j * 3 + k) * C
                        value = part_ref[n : n + C, :]
                        if kind:
                            m = ((2 - i) * 9 + (2 - j) * 3 + k) * C
                            value = value.T
                        else:
                            m = (i * 9 + j * 3 + 2 - k) * C
                        whole[m : m + C, :] = value.astype(F32)
                copy(kind, 2 - i if kind else i).start()
            for i in range(3):
                copy(kind, i).wait()


def write(half, where, part, targets=()):
    return pl.pallas_call(
        lambda *refs: write_kernel(half, *refs),
        out_shape=[jax.ShapeDtypeStruct((ROWS, C), F32)] * 2,
        in_specs=[SMEM, VMEM] + [ANY] * len(targets),
        out_specs=[ANY, ANY],
        input_output_aliases={2 + n: n for n in range(len(targets))},
        scratch_shapes=[pltpu.VMEM((ROWS, C), F32), pltpu.SemaphoreType.DMA((3,))],
        compiler_params=pltpu.CompilerParams(vmem_limit_bytes=8 << 20),
        cost_estimate=pl.CostEstimate(flops=0, bytes_accessed=3 << 20, transcendentals=0),
    )(where, part, *targets)


def body(quantized, exponents, out_grad, kernel_one, kernel_two):
    tm = lax.axis_index("tm")
    index = lax.axis_index("height")
    core = tm % 2
    odd = index % 2 == 1
    where = jnp.stack([core, tm, index % 2]).astype(jnp.int32)
    one = kernel_one.reshape(27, C, C)
    two = kernel_two.reshape(27, C, C)
    nine = one.reshape(9, 3 * C, C)
    block = (2, 2, C, C)

    def met(near, far):
        inside = jnp.where(odd, index < HEIGHT - 1, index > 0)
        far = lax.optimization_barrier(jnp.where(inside, far, 0))
        before = jnp.where(odd, near, far)
        after = jnp.where(odd, far, near)
        return before, after

    def band(before, value, after):
        return jnp.concatenate([before[:, None], value, after[:, None]], axis=1)

    scale = jnp.exp2(exponents.astype(F32))
    scale = jnp.repeat(jnp.transpose(scale, (1, 2, 0)), C // 4, axis=2)
    scale = jnp.stack([scale, jnp.ones_like(scale)])[:, :, :, None, :]
    both = lax.optimization_barrier(jnp.stack([quantized, out_grad]))
    both = (both.astype(F32) * scale).astype(BF)
    pair = (4, C, C)
    near = send(jnp.where(odd, both[:, :, 0], both[:, :, 1]).reshape(pair), height_pairs(False))
    far = send(jnp.where(odd, both[:, :, 1], both[:, :, 0]).reshape(pair), height_pairs(True))
    near_own = send(both, tm_pairs(True))
    far_own = send(jnp.where(core == 0, both[1], both[0]), tm_pairs(False))
    before, after = met(near, far)
    margin = jnp.stack([before.reshape(2, 2, C, C), after.reshape(2, 2, C, C)], axis=2)
    near_margin = send(margin, tm_pairs(True))
    far_margin = send(jnp.where(core == 0, margin[1], margin[0]), tm_pairs(False))
    slab = (2, 4, C, 3 * C)
    flipped = (2, 3, C, 2 * C)
    half = 2 * 27 * C * C * 512
    middle, pre, hid = call(
        own_kernel,
        [(flipped, BF), ((512, C), F32), ((512, C), F32)],
        [where, both, margin, nine, two],
        specs=[SMEM] + [VMEM] * 4,
        scratch=[pltpu.VMEM(slab, BF), pltpu.VMEM(slab, BF)],
        flops=half,
        limit=16,
    )
    beside = [near_own, near_margin, far_own, far_margin]
    stay, leave, pre_grad = call(
        rest_kernel,
        [(block, BF)] * 3,
        [where, *beside, pre, hid, nine, two],
        specs=[SMEM] + [VMEM] * 8,
        scratch=[pltpu.VMEM(slab, BF), pltpu.VMEM(slab, BF)],
        flops=half,
        limit=16,
    )
    low, high = call(
        turn_kernel,
        [(flipped, BF)] * 2,
        [where, *beside],
        specs=[SMEM] + [VMEM] * 4,
        limit=16,
    )
    got = send(leave, SIBLING)
    (total,) = call(
        sums_kernel,
        [((ROWS, C), BF)],
        [where, stay, got, low, middle, high],
        specs=[SMEM] + [VMEM] * 5,
        out_specs=[ANY],
        scratch=[
            pltpu.VMEM((4, 2 * C, 3 * C), BF),
            pltpu.VMEM((ROWS, C), BF),
            pltpu.SemaphoreType.DMA((3,)),
        ],
        flops=2 * half,
        limit=16,
    )
    near = send(jnp.where(odd, pre_grad[:, 0], pre_grad[:, 1]), height_pairs(False))
    far = send(jnp.where(odd, pre_grad[:, 1], pre_grad[:, 0]), height_pairs(True))
    before, after = met(near, far)
    total = jnp.sum(exchange(total.reshape(16, PART, C)).astype(F32), axis=0).astype(BF)
    total, before, after = lax.optimization_barrier((total, before, after))
    pre_banded = band(before, pre_grad, after)
    pre_near = send(pre_banded, tm_pairs(True))
    pre_far = send(pre_banded, tm_pairs(False))
    other = send(total, flip_pairs(128))
    total = total.astype(F32) + other.astype(F32)
    total = total.astype(BF)
    others = [send(total, flip_pairs(16 * n)) for n in (1, 3, 2)]
    (in_grad,) = call(
        in_grad_kernel,
        [(block, BF)],
        [where, pre_near, pre_far, pre_banded, one],
        specs=[SMEM] + [VMEM] * 4,
        scratch=[pltpu.VMEM((4, 4, C, 3 * C), BF)],
        flops=2 * 27 * C * C * 512,
    )
    others, in_grad = lax.optimization_barrier((others, in_grad))
    total, *others = (part.astype(F32) for part in (total, *others))
    factor = 1.0 / math.sqrt(8 * 128 * 128)
    total = (((total + others[0]) + (others[1] + others[2])) * factor).astype(BF)
    mine = exchange(jnp.broadcast_to(total[None], (16, PART, C))).reshape(ROWS, C)
    theirs = send(mine, SIBLING)
    totals = write(0, where, mine)
    one_total, two_total = write(1, where, theirs, totals)
    shape = (3, 3, 3, C, C)
    return (in_grad, one_total.reshape(shape), two_total.reshape(shape))


def solution(mesh):
    placed = (
        P("tm", "height", None, None),
        P(None, "tm", "height"),
        P("tm", "height", None, None),
        P(),
        P(),
    )
    return jax.shard_map(
        body,
        mesh=mesh,
        in_specs=placed,
        out_specs=(P("tm", "height", None, None), P(), P()),
        check_vma=False,
    )
```

```python
import math

import jax
import jax.numpy as jnp
from jax import lax
from jax.experimental import pallas as pl
from jax.experimental.pallas import tpu as pltpu
from jax.sharding import PartitionSpec as P

BF = jnp.bfloat16
F32 = jnp.float32
AXES = ("tm", "height")
TM, HEIGHT = 4, 64
COUNT = TM * HEIGHT
C = 128
ROWS = 27 * C
PART = ROWS // 16


def tm_pairs(first):
    pairs = []
    for tm in range(TM):
        for h in range(HEIGHT):
            if first:
                pairs.append((tm * HEIGHT + h, (tm ^ 1) * HEIGHT + h))
            elif tm in (1, 2):
                pairs.append((tm * HEIGHT + h, (3 - tm) * HEIGHT + h))
            else:
                pairs.append((tm * HEIGHT + h, tm * HEIGHT + (h ^ 1)))
    return pairs


def height_pairs(odd):
    pairs = []
    for tm in range(TM):
        for h in range(HEIGHT):
            up = (h % 2 == 1) if odd else (h % 2 == 0)
            other = h + 1 if up else h - 1
            if 0 <= other < HEIGHT:
                pairs.append((tm * HEIGHT + h, tm * HEIGHT + other))
            else:
                pairs.append((tm * HEIGHT + h, (tm ^ 1) * HEIGHT + h))
    return pairs


def flip_pairs(mask):
    return [(d, d ^ mask) for d in range(COUNT)]


SIBLING = flip_pairs(64)
PLANE = [[base + (n + 10) % 16 for n in range(16)] for base in range(0, COUNT, 16)]


def send(value, pairs):
    return lax.ppermute(value, AXES, pairs)


def exchange(value):
    return lax.all_to_all(value, AXES, 0, 0, axis_index_groups=PLANE, tiled=True)


VMEM = pl.BlockSpec(memory_space=pltpu.VMEM)
SMEM = pl.BlockSpec(memory_space=pltpu.SMEM)
ANY = pl.BlockSpec(memory_space=pl.ANY)


def call(kernel, outs, ins, scratch=(), specs=None, out_specs=None, flops=0, moved=1 << 20, limit=8):
    return pl.pallas_call(
        kernel,
        out_shape=[jax.ShapeDtypeStruct(shape, kind) for shape, kind in outs],
        in_specs=specs or [VMEM] * len(ins),
        out_specs=out_specs or [VMEM] * len(outs),
        scratch_shapes=list(scratch),
        compiler_params=pltpu.CompilerParams(vmem_limit_bytes=limit << 20),
        cost_estimate=pl.CostEstimate(flops=flops, bytes_accessed=moved, transcendentals=0),
    )(*ins)


def columns(value):
    wide = value.astype(F32)
    row = lax.broadcasted_iota(jnp.int32, wide.shape, 0)
    before = jnp.where(row == 0, 0.0, pltpu.roll(wide, 1, 0)).astype(BF)
    after = jnp.where(row == 127, 0.0, pltpu.roll(wide, 127, 0)).astype(BF)
    return before, value, after


def dot(a, b):
    return lax.dot_general(a, b, (((1,), (0,)), ((), ())), preferred_element_type=F32)


def dot_nt(a, b):
    return lax.dot_general(a, b, (((1,), (1,)), ((), ())), preferred_element_type=F32)


def turned(kernel_ref, i, j):
    base = (2 - i) * 9 + (2 - j) * 3
    return jnp.concatenate([kernel_ref[base + 2], kernel_ref[base + 1], kernel_ref[base]], axis=1)


def fill(slab, t, r, value):
    for k, part in enumerate(columns(value)):
        slab[t, r, :, k * C : (k + 1) * C] = part


def fill_turned(turned_ref, t, r, value):
    flipped = value.T
    if r < 3:
        turned_ref[t, r, :, 0:C] = flipped
    if r > 0:
        turned_ref[t, r - 1, :, C : 2 * C] = flipped


def rows_of(slab, frames, j):
    return slab[frames, j : j + 2].reshape(-1, slab.shape[3])


BOTH, FIRST, SECOND = slice(0, 2), slice(0, 1), slice(1, 2)


def own_kernel(
    place_ref, value_ref, margin_ref, one_ref, two_ref,
    turned_ref, pre_ref, hid_ref, slab_i, slab_g,
):
    core = place_ref[0]
    for t in range(2):
        for r in range(4):
            first, second = (
                value_ref[n, t, r - 1] if 0 < r < 3 else margin_ref[n, t, r // 3] for n in range(2)
            )
            fill(slab_i, t, r, first)
            fill(slab_g, t, r, second)
            fill_turned(turned_ref, t, r, jnp.where(core == 0, first, second).astype(BF))
    pre = jnp.zeros((512, C), F32)
    hid = jnp.zeros((512, C), F32)
    pre_1 = jnp.zeros((256, C), F32)
    hid_0 = jnp.zeros((256, C), F32)
    for j in range(3):
        pre += dot(rows_of(slab_i, BOTH, j), one_ref[6 + j])
        pre_1 += dot(rows_of(slab_i, FIRST, j), one_ref[3 + j])
        hid += dot_nt(rows_of(slab_g, BOTH, j), turned(two_ref, 0, j))
        hid_0 += dot_nt(rows_of(slab_g, SECOND, j), turned(two_ref, 1, j))
    pre_ref[0:256] = pre[0:256]
    pre_ref[256:512] = pre[256:512] + pre_1
    hid_ref[0:256] = hid[0:256] + hid_0
    hid_ref[256:512] = hid[256:512]


def pick(own_ref, margin_ref, t, r, *n):
    return own_ref[(*n, t, r - 1)] if 0 < r < 3 else margin_ref[(*n, t, r // 3)]


def rest_kernel(
    place_ref, near_own, near_margin, far_own, far_margin, pre_ref, hid_ref, one_ref, two_ref,
    stay_ref, leave_ref, pre_grad_ref, past_i, later_g,
):
    core = place_ref[0]
    for t in range(2):
        for r in range(4):
            far = pick(far_own, far_margin, t, r)
            value = jnp.where(core == 1, pick(near_own, near_margin, t, r, 0), far)
            fill(past_i, t, r, jnp.where(place_ref[1] > 0, value, 0).astype(BF))
            value = jnp.where(core == 0, pick(near_own, near_margin, t, r, 1), far)
            fill(later_g, t, r, jnp.where(place_ref[1] < TM - 1, value, 0).astype(BF))
    pre = pre_ref[...]
    hid = hid_ref[...]
    pre_0 = jnp.zeros((256, C), F32)
    hid_1 = jnp.zeros((256, C), F32)
    for j in range(3):
        pre += dot(rows_of(past_i, BOTH, j), one_ref[j])
        pre_0 += dot(rows_of(past_i, SECOND, j), one_ref[3 + j])
        hid += dot_nt(rows_of(later_g, BOTH, j), turned(two_ref, 2, j))
        hid_1 += dot_nt(rows_of(later_g, FIRST, j), turned(two_ref, 1, j))
    pre = jnp.concatenate([pre[0:256] + pre_0, pre[256:512]], axis=0)
    hid = jnp.concatenate([hid[0:256], hid[256:512] + hid_1], axis=0)
    gate = 1.0 / (1.0 + jnp.exp(-pre))
    hidden = (pre * gate).astype(BF).reshape(2, 2, C, C)
    pre_grad = (hid * gate * (1.0 + pre * (1.0 - gate))).astype(BF).reshape(2, 2, C, C)
    pre_grad_ref[...] = pre_grad
    stay_ref[...] = jnp.where(core == 0, pre_grad, hidden).astype(BF)
    leave_ref[...] = jnp.where(core == 0, hidden, pre_grad).astype(BF)


def turn_kernel(place_ref, near_own, near_margin, far_own, far_margin, low_ref, high_ref):
    core = place_ref[0]
    inner = (place_ref[1] == 1) | (place_ref[1] == 2)
    for t in range(2):
        for r in range(4):
            far = jnp.where(inner, pick(far_own, far_margin, t, r), 0).astype(BF)
            first = pick(near_own, near_margin, t, r, 0)
            second = pick(near_own, near_margin, t, r, 1)
            fill_turned(low_ref, t, r, jnp.where(core == 0, far, second).astype(BF))
            fill_turned(high_ref, t, r, jnp.where(core == 0, first, far).astype(BF))


def sums_kernel(place_ref, stay_ref, got_ref, low_ref, own_ref, high_ref, out_hbm, slab, out_ref, sems):
    core = place_ref[0]
    for t in range(4):
        for r in range(2):
            early, late = (stay_ref, got_ref) if t < 2 else (got_ref, stay_ref)
            value = jnp.where(core == 0, early[t % 2, r], late[t % 2, r]).astype(BF)
            for k, part in enumerate(columns(value)):
                slab[t, r * C : (r + 1) * C, k * C : (k + 1) * C] = part
    frames = [ref.at[t] for ref in (low_ref, own_ref, high_ref) for t in range(2)]
    copies = []
    for i in range(3):
        total = jnp.zeros((3 * C, 3 * C), F32)
        for t in range(4):
            total += dot(frames[i + t][...].reshape(3 * C, 2 * C), slab[t])
        total = total.astype(BF)
        for j in range(3):
            for k in range(3):
                n = i * 9 + j * 3 + k
                out_ref[n * C : (n + 1) * C, :] = total[j * C : (j + 1) * C, k * C : (k + 1) * C]
        rows = pl.ds(i * (ROWS // 3), ROWS // 3)
        copies.append(pltpu.make_async_copy(out_ref.at[rows, :], out_hbm.at[rows, :], sems.at[i]))
        copies[-1].start()
    for copy in copies:
        copy.wait()


def in_grad_kernel(place_ref, later_ref, own_ref, one_ref, out_ref, slab):
    def later(t, r):
        return jnp.where(place_ref[1] < TM - 1, later_ref[t, r], 0).astype(BF)

    for t in range(4):
        for r in range(4):
            value = own_ref[t, r] if t < 2 else later(t - 2, r)
            for k, part in enumerate(columns(value)):
                slab[t, r, :, k * C : (k + 1) * C] = part
    total = jnp.zeros((512, C), F32)
    for i in range(3):
        for j in range(3):
            total += dot_nt(slab[i : i + 2, j : j + 2].reshape(512, 3 * C), turned(one_ref, i, j))
    out_ref[...] = total.astype(BF).reshape(2, 2, C, C)


def write_kernel(half, place_ref, part_ref, *refs):
    targets, whole, sems = refs[-4:-2], refs[-2], refs[-1]
    third = ROWS // 3

    def copy(kind, i):
        rows = pl.ds(i * third, third)
        return pltpu.make_async_copy(whole.at[rows, :], targets[kind].at[rows, :], sems.at[i])

    for kind in range(2):

        @pl.when(place_ref[0] == (kind + half) % 2)
        def _():
            for i in range(3):
                for j in range(3):
                    for k in range(3):
                        n = (i * 9 + j * 3 + k) * C
                        value = part_ref[n : n + C, :]
                        if kind:
                            m = ((2 - i) * 9 + (2 - j) * 3 + k) * C
                            value = value.T
                        else:
                            m = (i * 9 + j * 3 + 2 - k) * C
                        whole[m : m + C, :] = value.astype(F32)
                copy(kind, 2 - i if kind else i).start()
            for i in range(3):
                copy(kind, i).wait()


def write(half, where, part, targets=()):
    return pl.pallas_call(
        lambda *refs: write_kernel(half, *refs),
        out_shape=[jax.ShapeDtypeStruct((ROWS, C), F32)] * 2,
        in_specs=[SMEM, VMEM] + [ANY] * len(targets),
        out_specs=[ANY, ANY],
        input_output_aliases={2 + n: n for n in range(len(targets))},
        scratch_shapes=[pltpu.VMEM((ROWS, C), F32), pltpu.SemaphoreType.DMA((3,))],
        compiler_params=pltpu.CompilerParams(vmem_limit_bytes=8 << 20),
        cost_estimate=pl.CostEstimate(flops=0, bytes_accessed=3 << 20, transcendentals=0),
    )(where, part, *targets)


def body(quantized, exponents, out_grad, kernel_one, kernel_two):
    tm = lax.axis_index("tm")
    index = lax.axis_index("height")
    core = tm % 2
    odd = index % 2 == 1
    where = jnp.stack([core, tm, index % 2]).astype(jnp.int32)
    one = kernel_one.reshape(27, C, C)
    two = kernel_two.reshape(27, C, C)
    nine = one.reshape(9, 3 * C, C)
    block = (2, 2, C, C)

    def met(near, far):
        inside = jnp.where(odd, index < HEIGHT - 1, index > 0)
        far = lax.optimization_barrier(jnp.where(inside, far, 0))
        before = jnp.where(odd, near, far)
        after = jnp.where(odd, far, near)
        return before, after

    def band(before, value, after):
        return jnp.concatenate([before[:, None], value, after[:, None]], axis=1)

    scale = jnp.exp2(exponents.astype(F32))
    scale = jnp.repeat(jnp.transpose(scale, (1, 2, 0)), C // 4, axis=2)
    scale = jnp.stack([scale, jnp.ones_like(scale)])[:, :, :, None, :]
    both = lax.optimization_barrier(jnp.stack([quantized, out_grad]))
    both = (both.astype(F32) * scale).astype(BF)
    pair = (4, C, C)
    near = send(jnp.where(odd, both[:, :, 0], both[:, :, 1]).reshape(pair), height_pairs(False))
    far = send(jnp.where(odd, both[:, :, 1], both[:, :, 0]).reshape(pair), height_pairs(True))
    near_own = send(both, tm_pairs(True))
    far_own = send(jnp.where(core == 0, both[1], both[0]), tm_pairs(False))
    before, after = met(near, far)
    margin = jnp.stack([before.reshape(2, 2, C, C), after.reshape(2, 2, C, C)], axis=2)
    near_margin = send(margin, tm_pairs(True))
    far_margin = send(jnp.where(core == 0, margin[1], margin[0]), tm_pairs(False))
    slab = (2, 4, C, 3 * C)
    flipped = (2, 3, C, 2 * C)
    half = 2 * 27 * C * C * 512
    middle, pre, hid = call(
        own_kernel,
        [(flipped, BF), ((512, C), F32), ((512, C), F32)],
        [where, both, margin, nine, two],
        specs=[SMEM] + [VMEM] * 4,
        scratch=[pltpu.VMEM(slab, BF), pltpu.VMEM(slab, BF)],
        flops=half,
        limit=16,
    )
    beside = [near_own, near_margin, far_own, far_margin]
    stay, leave, pre_grad = call(
        rest_kernel,
        [(block, BF)] * 3,
        [where, *beside, pre, hid, nine, two],
        specs=[SMEM] + [VMEM] * 8,
        scratch=[pltpu.VMEM(slab, BF), pltpu.VMEM(slab, BF)],
        flops=half,
        limit=16,
    )
    low, high = call(
        turn_kernel,
        [(flipped, BF)] * 2,
        [where, *beside],
        specs=[SMEM] + [VMEM] * 4,
        limit=16,
    )
    got = send(leave, SIBLING)
    (total,) = call(
        sums_kernel,
        [((ROWS, C), BF)],
        [where, stay, got, low, middle, high],
        specs=[SMEM] + [VMEM] * 5,
        out_specs=[ANY],
        scratch=[
            pltpu.VMEM((4, 2 * C, 3 * C), BF),
            pltpu.VMEM((ROWS, C), BF),
            pltpu.SemaphoreType.DMA((3,)),
        ],
        flops=2 * half,
        limit=16,
    )
    near = send(jnp.where(odd, pre_grad[:, 0], pre_grad[:, 1]), height_pairs(False))
    far = send(jnp.where(odd, pre_grad[:, 1], pre_grad[:, 0]), height_pairs(True))
    before, after = met(near, far)
    total = jnp.sum(exchange(total.reshape(16, PART, C)).astype(F32), axis=0).astype(BF)
    total, before, after = lax.optimization_barrier((total, before, after))
    pre_banded = band(before, pre_grad, after)
    pre_later = send(pre_banded, [(d, (d - HEIGHT) % COUNT) for d in range(COUNT)])
    other = send(total, flip_pairs(128))
    total = total.astype(F32) + other.astype(F32)
    total = total.astype(BF)
    others = [send(total, flip_pairs(16 * n)) for n in (1, 3, 2)]
    (in_grad,) = call(
        in_grad_kernel,
        [(block, BF)],
        [where, pre_later, pre_banded, one],
        specs=[SMEM] + [VMEM] * 3,
        scratch=[pltpu.VMEM((4, 4, C, 3 * C), BF)],
        flops=2 * 27 * C * C * 512,
    )
    others, in_grad = lax.optimization_barrier((others, in_grad))
    total, *others = (part.astype(F32) for part in (total, *others))
    factor = 1.0 / math.sqrt(8 * 128 * 128)
    total = (((total + others[0]) + (others[1] + others[2])) * factor).astype(BF)
    mine = exchange(jnp.broadcast_to(total[None], (16, PART, C))).reshape(ROWS, C)
    theirs = send(mine, SIBLING)
    totals = write(0, where, mine)
    one_total, two_total = write(1, where, theirs, totals)
    shape = (3, 3, 3, C, C)
    return (in_grad, one_total.reshape(shape), two_total.reshape(shape))


def solution(mesh):
    placed = (
        P("tm", "height", None, None),
        P(None, "tm", "height"),
        P("tm", "height", None, None),
        P(),
        P(),
    )
    return jax.shard_map(
        body,
        mesh=mesh,
        in_specs=placed,
        out_specs=(P("tm", "height", None, None), P(), P()),
        check_vma=False,
    )
```

```python
import math

import jax
import jax.numpy as jnp
from jax import lax
from jax.experimental import pallas as pl
from jax.experimental.pallas import tpu as pltpu
from jax.sharding import PartitionSpec as P

BF = jnp.bfloat16
F32 = jnp.float32
AXES = ("tm", "height")
TM, HEIGHT = 4, 64
COUNT = TM * HEIGHT
C = 128
ROWS = 27 * C
PART = ROWS // 16


def tm_pairs(first):
    pairs = []
    for tm in range(TM):
        for h in range(HEIGHT):
            if first:
                pairs.append((tm * HEIGHT + h, (tm ^ 1) * HEIGHT + h))
            elif tm in (1, 2):
                pairs.append((tm * HEIGHT + h, (3 - tm) * HEIGHT + h))
            else:
                pairs.append((tm * HEIGHT + h, tm * HEIGHT + (h ^ 1)))
    return pairs


def height_pairs(odd):
    pairs = []
    for tm in range(TM):
        for h in range(HEIGHT):
            up = (h % 2 == 1) if odd else (h % 2 == 0)
            other = h + 1 if up else h - 1
            if 0 <= other < HEIGHT:
                pairs.append((tm * HEIGHT + h, tm * HEIGHT + other))
            else:
                pairs.append((tm * HEIGHT + h, (tm ^ 1) * HEIGHT + h))
    return pairs


def flip_pairs(mask):
    return [(d, d ^ mask) for d in range(COUNT)]


SIBLING = flip_pairs(64)
PLANE = [[base + (n + 10) % 16 for n in range(16)] for base in range(0, COUNT, 16)]


def send(value, pairs):
    return lax.ppermute(value, AXES, pairs)


def exchange(value):
    return lax.all_to_all(value, AXES, 0, 0, axis_index_groups=PLANE, tiled=True)


VMEM = pl.BlockSpec(memory_space=pltpu.VMEM)
SMEM = pl.BlockSpec(memory_space=pltpu.SMEM)
ANY = pl.BlockSpec(memory_space=pl.ANY)


def call(kernel, outs, ins, scratch=(), specs=None, out_specs=None, flops=0, moved=1 << 20, limit=8):
    return pl.pallas_call(
        kernel,
        out_shape=[jax.ShapeDtypeStruct(shape, kind) for shape, kind in outs],
        in_specs=specs or [VMEM] * len(ins),
        out_specs=out_specs or [VMEM] * len(outs),
        scratch_shapes=list(scratch),
        compiler_params=pltpu.CompilerParams(vmem_limit_bytes=limit << 20),
        cost_estimate=pl.CostEstimate(flops=flops, bytes_accessed=moved, transcendentals=0),
    )(*ins)


def columns(value):
    wide = value.astype(F32)
    row = lax.broadcasted_iota(jnp.int32, wide.shape, 0)
    before = jnp.where(row == 0, 0.0, pltpu.roll(wide, 1, 0)).astype(BF)
    after = jnp.where(row == 127, 0.0, pltpu.roll(wide, 127, 0)).astype(BF)
    return before, value, after


def dot(a, b):
    return lax.dot_general(a, b, (((1,), (0,)), ((), ())), preferred_element_type=F32)


def dot_nt(a, b):
    return lax.dot_general(a, b, (((1,), (1,)), ((), ())), preferred_element_type=F32)


def turned(kernel_ref, i, j):
    base = (2 - i) * 9 + (2 - j) * 3
    return jnp.concatenate([kernel_ref[base + 2], kernel_ref[base + 1], kernel_ref[base]], axis=1)


def fill(slab, t, r, value):
    for k, part in enumerate(columns(value)):
        slab[t, r, :, k * C : (k + 1) * C] = part


def fill_turned(turned_ref, t, r, value):
    flipped = value.T
    if r < 3:
        turned_ref[t, r, :, 0:C] = flipped
    if r > 0:
        turned_ref[t, r - 1, :, C : 2 * C] = flipped


def rows_of(slab, frames, j):
    return slab[frames, j : j + 2].reshape(-1, slab.shape[3])


BOTH, FIRST, SECOND = slice(0, 2), slice(0, 1), slice(1, 2)


def own_kernel(
    place_ref, value_ref, margin_ref, one_ref, two_ref,
    turned_ref, pre_ref, hid_ref, slab_i, slab_g,
):
    core = place_ref[0]
    for t in range(2):
        for r in range(4):
            first, second = (
                value_ref[n, t, r - 1] if 0 < r < 3 else margin_ref[n, t, r // 3] for n in range(2)
            )
            fill(slab_i, t, r, first)
            fill(slab_g, t, r, second)
            fill_turned(turned_ref, t, r, jnp.where(core == 0, first, second).astype(BF))
    pre = jnp.zeros((512, C), F32)
    hid = jnp.zeros((512, C), F32)
    pre_1 = jnp.zeros((256, C), F32)
    hid_0 = jnp.zeros((256, C), F32)
    for j in range(3):
        pre += dot(rows_of(slab_i, BOTH, j), one_ref[6 + j])
        pre_1 += dot(rows_of(slab_i, FIRST, j), one_ref[3 + j])
        hid += dot_nt(rows_of(slab_g, BOTH, j), turned(two_ref, 0, j))
        hid_0 += dot_nt(rows_of(slab_g, SECOND, j), turned(two_ref, 1, j))
    pre_ref[0:256] = pre[0:256]
    pre_ref[256:512] = pre[256:512] + pre_1
    hid_ref[0:256] = hid[0:256] + hid_0
    hid_ref[256:512] = hid[256:512]


def pick(own_ref, margin_ref, t, r, *n):
    return own_ref[(*n, t, r - 1)] if 0 < r < 3 else margin_ref[(*n, t, r // 3)]


def rest_kernel(
    place_ref, near_own, near_margin, far_own, far_margin, pre_ref, hid_ref, one_ref, two_ref,
    stay_ref, leave_ref, pre_grad_ref, past_i, later_g,
):
    core = place_ref[0]
    for t in range(2):
        for r in range(4):
            far = pick(far_own, far_margin, t, r)
            value = jnp.where(core == 1, pick(near_own, near_margin, t, r, 0), far)
            fill(past_i, t, r, jnp.where(place_ref[1] > 0, value, 0).astype(BF))
            value = jnp.where(core == 0, pick(near_own, near_margin, t, r, 1), far)
            fill(later_g, t, r, jnp.where(place_ref[1] < TM - 1, value, 0).astype(BF))
    pre = pre_ref[...]
    hid = hid_ref[...]
    pre_0 = jnp.zeros((256, C), F32)
    hid_1 = jnp.zeros((256, C), F32)
    for j in range(3):
        pre += dot(rows_of(past_i, BOTH, j), one_ref[j])
        pre_0 += dot(rows_of(past_i, SECOND, j), one_ref[3 + j])
        hid += dot_nt(rows_of(later_g, BOTH, j), turned(two_ref, 2, j))
        hid_1 += dot_nt(rows_of(later_g, FIRST, j), turned(two_ref, 1, j))
    pre = jnp.concatenate([pre[0:256] + pre_0, pre[256:512]], axis=0)
    hid = jnp.concatenate([hid[0:256], hid[256:512] + hid_1], axis=0)
    gate = 1.0 / (1.0 + jnp.exp(-pre))
    hidden = (pre * gate).astype(BF).reshape(2, 2, C, C)
    pre_grad = (hid * gate * (1.0 + pre * (1.0 - gate))).astype(BF).reshape(2, 2, C, C)
    pre_grad_ref[...] = pre_grad
    stay_ref[...] = jnp.where(core == 0, pre_grad, hidden).astype(BF)
    leave_ref[...] = jnp.where(core == 0, hidden, pre_grad).astype(BF)


def turn_kernel(place_ref, near_own, near_margin, far_own, far_margin, low_ref, high_ref):
    core = place_ref[0]
    inner = (place_ref[1] == 1) | (place_ref[1] == 2)
    for t in range(2):
        for r in range(4):
            far = jnp.where(inner, pick(far_own, far_margin, t, r), 0).astype(BF)
            first = pick(near_own, near_margin, t, r, 0)
            second = pick(near_own, near_margin, t, r, 1)
            fill_turned(low_ref, t, r, jnp.where(core == 0, far, second).astype(BF))
            fill_turned(high_ref, t, r, jnp.where(core == 0, first, far).astype(BF))


def sums_kernel(place_ref, stay_ref, got_ref, low_ref, own_ref, high_ref, out_hbm, slab, out_ref, sems):
    core = place_ref[0]
    for t in range(4):
        for r in range(2):
            early, late = (stay_ref, got_ref) if t < 2 else (got_ref, stay_ref)
            value = jnp.where(core == 0, early[t % 2, r], late[t % 2, r]).astype(BF)
            for k, part in enumerate(columns(value)):
                slab[t, r * C : (r + 1) * C, k * C : (k + 1) * C] = part
    frames = [ref.at[t] for ref in (low_ref, own_ref, high_ref) for t in range(2)]
    copies = []
    for i in range(3):
        total = jnp.zeros((3 * C, 3 * C), F32)
        for t in range(4):
            total += dot(frames[i + t][...].reshape(3 * C, 2 * C), slab[t])
        total = total.astype(BF)
        for j in range(3):
            for k in range(3):
                n = i * 9 + j * 3 + k
                out_ref[n * C : (n + 1) * C, :] = total[j * C : (j + 1) * C, k * C : (k + 1) * C]
        rows = pl.ds(i * (ROWS // 3), ROWS // 3)
        copies.append(pltpu.make_async_copy(out_ref.at[rows, :], out_hbm.at[rows, :], sems.at[i]))
        copies[-1].start()
    for copy in copies:
        copy.wait()


def in_grad_kernel(place_ref, later_ref, own_ref, one_ref, out_ref, slab):
    def later(t, r):
        return jnp.where(place_ref[1] < TM - 1, later_ref[t, r], 0).astype(BF)

    for t in range(4):
        for r in range(4):
            value = own_ref[t, r] if t < 2 else later(t - 2, r)
            for k, part in enumerate(columns(value)):
                slab[t, r, :, k * C : (k + 1) * C] = part
    total = jnp.zeros((512, C), F32)
    for i in range(3):
        for j in range(3):
            total += dot_nt(slab[i : i + 2, j : j + 2].reshape(512, 3 * C), turned(one_ref, i, j))
    out_ref[...] = total.astype(BF).reshape(2, 2, C, C)


def write_kernel(half, place_ref, part_ref, *refs):
    targets, whole, sems = refs[-4:-2], refs[-2], refs[-1]
    ninth = ROWS // 9

    def copy(kind, i):
        rows = pl.ds(i * ninth, ninth)
        return pltpu.make_async_copy(whole.at[rows, :], targets[kind].at[rows, :], sems.at[i])

    for kind in range(2):

        @pl.when(place_ref[0] == (kind + half) % 2)
        def _():
            for i in range(3):
                for j in range(3):
                    for k in range(3):
                        n = (i * 9 + j * 3 + k) * C
                        value = part_ref[n : n + C, :]
                        if kind:
                            m = ((2 - i) * 9 + (2 - j) * 3 + k) * C
                            value = value.T
                        else:
                            m = (i * 9 + j * 3 + 2 - k) * C
                        whole[m : m + C, :] = value.astype(F32)
                    copy(kind, 8 - i * 3 - j if kind else i * 3 + j).start()
            for i in range(9):
                copy(kind, i).wait()


def write(half, where, part, targets=()):
    return pl.pallas_call(
        lambda *refs: write_kernel(half, *refs),
        out_shape=[jax.ShapeDtypeStruct((ROWS, C), F32)] * 2,
        in_specs=[SMEM, VMEM] + [ANY] * len(targets),
        out_specs=[ANY, ANY],
        input_output_aliases={2 + n: n for n in range(len(targets))},
        scratch_shapes=[pltpu.VMEM((ROWS, C), F32), pltpu.SemaphoreType.DMA((9,))],
        compiler_params=pltpu.CompilerParams(vmem_limit_bytes=8 << 20),
        cost_estimate=pl.CostEstimate(flops=0, bytes_accessed=3 << 20, transcendentals=0),
    )(where, part, *targets)


def body(quantized, exponents, out_grad, kernel_one, kernel_two):
    tm = lax.axis_index("tm")
    index = lax.axis_index("height")
    core = tm % 2
    odd = index % 2 == 1
    where = jnp.stack([core, tm, index % 2]).astype(jnp.int32)
    one = kernel_one.reshape(27, C, C)
    two = kernel_two.reshape(27, C, C)
    nine = one.reshape(9, 3 * C, C)
    block = (2, 2, C, C)

    def met(near, far):
        inside = jnp.where(odd, index < HEIGHT - 1, index > 0)
        far = lax.optimization_barrier(jnp.where(inside, far, 0))
        before = jnp.where(odd, near, far)
        after = jnp.where(odd, far, near)
        return before, after

    def band(before, value, after):
        return jnp.concatenate([before[:, None], value, after[:, None]], axis=1)

    scale = jnp.exp2(exponents.astype(F32))
    scale = jnp.repeat(jnp.transpose(scale, (1, 2, 0)), C // 4, axis=2)
    scale = jnp.stack([scale, jnp.ones_like(scale)])[:, :, :, None, :]
    both = lax.optimization_barrier(jnp.stack([quantized, out_grad]))
    both = (both.astype(F32) * scale).astype(BF)
    pair = (4, C, C)
    near = send(jnp.where(odd, both[:, :, 0], both[:, :, 1]).reshape(pair), height_pairs(False))
    far = send(jnp.where(odd, both[:, :, 1], both[:, :, 0]).reshape(pair), height_pairs(True))
    near_own = send(both, tm_pairs(True))
    far_own = send(jnp.where(core == 0, both[1], both[0]), tm_pairs(False))
    before, after = met(near, far)
    margin = jnp.stack([before.reshape(2, 2, C, C), after.reshape(2, 2, C, C)], axis=2)
    near_margin = send(margin, tm_pairs(True))
    far_margin = send(jnp.where(core == 0, margin[1], margin[0]), tm_pairs(False))
    slab = (2, 4, C, 3 * C)
    flipped = (2, 3, C, 2 * C)
    half = 2 * 27 * C * C * 512
    middle, pre, hid = call(
        own_kernel,
        [(flipped, BF), ((512, C), F32), ((512, C), F32)],
        [where, both, margin, nine, two],
        specs=[SMEM] + [VMEM] * 4,
        scratch=[pltpu.VMEM(slab, BF), pltpu.VMEM(slab, BF)],
        flops=half,
        limit=16,
    )
    beside = [near_own, near_margin, far_own, far_margin]
    stay, leave, pre_grad = call(
        rest_kernel,
        [(block, BF)] * 3,
        [where, *beside, pre, hid, nine, two],
        specs=[SMEM] + [VMEM] * 8,
        scratch=[pltpu.VMEM(slab, BF), pltpu.VMEM(slab, BF)],
        flops=half,
        limit=16,
    )
    low, high = call(
        turn_kernel,
        [(flipped, BF)] * 2,
        [where, *beside],
        specs=[SMEM] + [VMEM] * 4,
        limit=16,
    )
    got = send(leave, SIBLING)
    (total,) = call(
        sums_kernel,
        [((ROWS, C), BF)],
        [where, stay, got, low, middle, high],
        specs=[SMEM] + [VMEM] * 5,
        out_specs=[ANY],
        scratch=[
            pltpu.VMEM((4, 2 * C, 3 * C), BF),
            pltpu.VMEM((ROWS, C), BF),
            pltpu.SemaphoreType.DMA((3,)),
        ],
        flops=2 * half,
        limit=16,
    )
    near = send(jnp.where(odd, pre_grad[:, 0], pre_grad[:, 1]), height_pairs(False))
    far = send(jnp.where(odd, pre_grad[:, 1], pre_grad[:, 0]), height_pairs(True))
    before, after = met(near, far)
    total = jnp.sum(exchange(total.reshape(16, PART, C)).astype(F32), axis=0).astype(BF)
    total, before, after = lax.optimization_barrier((total, before, after))
    pre_banded = band(before, pre_grad, after)
    pre_later = send(pre_banded, [(d, (d - HEIGHT) % COUNT) for d in range(COUNT)])
    other = send(total, flip_pairs(128))
    total = total.astype(F32) + other.astype(F32)
    total = total.astype(BF)
    others = [send(total, flip_pairs(16 * n)) for n in (1, 3, 2)]
    (in_grad,) = call(
        in_grad_kernel,
        [(block, BF)],
        [where, pre_later, pre_banded, one],
        specs=[SMEM] + [VMEM] * 3,
        scratch=[pltpu.VMEM((4, 4, C, 3 * C), BF)],
        flops=2 * 27 * C * C * 512,
    )
    others, in_grad = lax.optimization_barrier((others, in_grad))
    total, *others = (part.astype(F32) for part in (total, *others))
    factor = 1.0 / math.sqrt(8 * 128 * 128)
    total = (((total + others[0]) + (others[1] + others[2])) * factor).astype(BF)
    mine = exchange(jnp.broadcast_to(total[None], (16, PART, C))).reshape(ROWS, C)
    theirs = send(mine, SIBLING)
    totals = write(0, where, mine)
    one_total, two_total = write(1, where, theirs, totals)
    shape = (3, 3, 3, C, C)
    return (in_grad, one_total.reshape(shape), two_total.reshape(shape))


def solution(mesh):
    placed = (
        P("tm", "height", None, None),
        P(None, "tm", "height"),
        P("tm", "height", None, None),
        P(),
        P(),
    )
    return jax.shard_map(
        body,
        mesh=mesh,
        in_specs=placed,
        out_specs=(P("tm", "height", None, None), P(), P()),
        check_vma=False,
    )
```
